256 devices in a mesh: chan: 64 (over z_hi, y, x), tm: 4 (over z_lo, core).
Axes of the slice: x: 4, y: 4, z: 8 (z_hi: 4, z_lo: 2; z = z_hi * 2 + z_lo), core: 2. Of those that a mesh axis runs over, the one named last changes fastest.
Arguments:
- records: bfloat16 [8192, 32, 1920], P('chan', 'tm'), may hold values from -6 to 6
- partners: int32 [64, 4], P('chan'), may hold values from -1 to 63, as said below
Outputs:
- stacked: float32 [64, 4, 128, 128], P('chan', None, 'tm')
The draws below stay inside these ranges and needn't reach their ends.
Inputs may be any that keep to these rules, and one draw needn't show every extreme that they name: Each row b lists distinct partner blocks b + k with 1 <= k <= 4 in increasing order, then -1 in the remaining slots; the number of partners differs from block to block, row 0 has 4, every block but the last has at least one, the last none.
All inputs are finite; a program needn't handle non-finite values.
Results may differ from the reference program's by a relative error of at most 0.0058.
Values may be sent and summed in bfloat16 or wider, within the bound.
A program may use at most 128 MiB of HBM per device.

```python
import math
import jax
import jax.numpy as jnp
from jax import lax

BLOCK_CH = 128
LEN = 1920
FREQ = 768
LAGS = 128
REACH = 4
BLOCKS = 64
CHANNELS = 8192
GROUPS = 32


def draw_partners(key, part):
    key = jax.random.fold_in(key, 7)
    count_key, score_key = jax.random.split(key)
    blocks = jnp.arange(BLOCKS, dtype=jnp.int32)[:, None]
    offsets = jnp.arange(1, REACH + 1, dtype=jnp.int32)[None, :]
    allowed = blocks + offsets <= BLOCKS - 1
    room = jnp.sum(allowed.astype(jnp.int32), axis=1)
    counts = jax.random.randint(count_key, (BLOCKS,), 1, REACH + 1)
    counts = counts.at[0].set(REACH)
    counts = jnp.minimum(counts, room)
    scores = jax.random.randint(score_key, (BLOCKS, REACH), 0, 1000) * REACH + (offsets - 1)
    scores = jnp.where(allowed, scores, 1000 * REACH + offsets)
    ordering = jnp.argsort(scores, axis=1, stable=True)
    chosen = jnp.take_along_axis(jnp.broadcast_to(offsets, (BLOCKS, REACH)), ordering, axis=1)
    keep = jnp.arange(REACH, dtype=jnp.int32)[None, :] < counts[:, None]
    picked = jnp.sort(jnp.where(keep, chosen, REACH + 1), axis=1)
    return jnp.where(picked <= REACH, blocks + picked, -1).astype(jnp.int32)


def steps_of(key, dims, cuts, least, largest):
    gain, own = 1.0, jax.random.fold_in(key, 6)
    for axis_at, shards_of in cuts:
        draws = jnp.exp(jax.random.uniform(jax.random.fold_in(own, axis_at), (shards_of,), jnp.float32, least / len(cuts), largest / len(cuts)))
        gain = gain * jnp.repeat(draws, dims[axis_at] // shards_of).reshape([-1 if axis == axis_at else 1 for axis in range(len(dims))])
    return gain


def noise(stream_key, extent, scale, most, cuts=(), held_as=jnp.bfloat16):
    values = jax.random.normal(stream_key, extent, jnp.float32) * scale
    if len(cuts) > 0:
        values = steps_of(stream_key, extent, cuts, -0.22, 0.18) * values
    return jnp.clip(values, min=-most, max=most).astype(held_as)


def setup_inputs(seed: int = 0) -> dict:
    seeds = jax.random.split(jax.random.key(seed), 3)
    return {
        "records": noise(seeds[0], (CHANNELS, GROUPS, LEN), 1.0, 6.0, ((0, 64), (1, 4))),
        "partners": draw_partners(jax.random.fold_in(seeds[2], 71), 0),
    }


def make_forward():
    times = jnp.arange(LEN, dtype=jnp.int32)[:, None]
    bins = jnp.arange(1, FREQ + 1, dtype=jnp.int32)[None, :]
    phase = times * bins % LEN
    angle = 2.0 * math.pi / LEN * phase.astype(jnp.float32)
    return jnp.concatenate([jnp.cos(angle), -jnp.sin(angle)], axis=1).astype(jnp.bfloat16)

def make_inverse():
    bins = jnp.arange(1, FREQ + 1, dtype=jnp.int32)[:, None]
    shifts = jnp.arange(LAGS, dtype=jnp.int32)[None, :] - LAGS // 2
    phase = bins * shifts % LEN
    angle = 2.0 * math.pi / LEN * phase.astype(jnp.float32)
    return jnp.concatenate([jnp.cos(angle), -jnp.sin(angle)], axis=0)

def whiten_block(block, forward):
    flat = block.reshape(-1, LEN)
    spectrum = jnp.dot(flat, forward, preferred_element_type=jnp.float32)
    real_part = spectrum[:, :FREQ]
    imag_part = spectrum[:, FREQ:]
    magnitude = jnp.sqrt(real_part * real_part + imag_part * imag_part)
    water_level = lax.optimization_barrier(jnp.mean(magnitude, axis=1, keepdims=True))
    denominator = magnitude + 0.1 * water_level + 1e-06
    whitened = jnp.concatenate([real_part / denominator, imag_part / denominator], axis=1)
    return whitened.astype(jnp.bfloat16).reshape(block.shape[0], block.shape[1], 2 * FREQ)

def cross_sum(left, right):
    left = left.astype(jnp.float32)
    right = right.astype(jnp.float32)
    left_real, left_imag = (left[..., :FREQ], left[..., FREQ:])
    right_real, right_imag = (right[..., :FREQ], right[..., FREQ:])
    real_sum = lax.optimization_barrier(jnp.sum(left_real * right_real + left_imag * right_imag, axis=1))
    imag_sum = lax.optimization_barrier(jnp.sum(left_imag * right_real - left_real * right_imag, axis=1))
    return jnp.concatenate([real_sum, imag_sum], axis=1)

def reference(records, partners):
    forward = make_forward()
    inverse = make_inverse()
    blocked = records.reshape(BLOCKS, BLOCK_CH, GROUPS, LEN)
    whitened_all = lax.map(lambda block: whiten_block(block, forward), blocked)
    norm_scale = 1.0 / math.sqrt(GROUPS * FREQ)

    def one_block(index):
        own = whitened_all[index]
        crosses = []
        for offset in range(1, REACH + 1):
            other = jnp.minimum(index + offset, BLOCKS - 1)
            valid = (index + offset <= BLOCKS - 1).astype(jnp.float32)
            crosses.append(cross_sum(own, whitened_all[other]) * valid)
        crosses = jnp.stack(crosses)
        lagged = jnp.einsum('kcf,fl->kcl', crosses, inverse, precision=lax.Precision.HIGHEST) * norm_scale
        offsets = partners[index] - index
        selector = (offsets[:, None] == jnp.arange(1, REACH + 1, dtype=jnp.int32)[None, :]).astype(jnp.float32)
        return jnp.einsum('jk,kcl->jcl', selector, lagged, precision=lax.Precision.HIGHEST)
    return lax.map(one_block, jnp.arange(BLOCKS, dtype=jnp.int32))
```

```python
import functools
import math

import jax
import jax.numpy as jnp
import numpy as np
from jax import lax
from jax.experimental import pallas as pl
from jax.experimental.pallas import tpu as pltpu
from jax.sharding import PartitionSpec as P

FREQ = 768
LAGS = 128
REACH = 4
LEN = 1920
ROW = 4
TM = 4
CHUNKS = 8
PIECES = 3
WIDE = FREQ // PIECES
MESH = pl.DeviceIdType.MESH
F32 = jnp.float32
BF16 = jnp.bfloat16


def forward_matrix():
    times = np.arange(LEN, dtype=np.int64)[:, None]
    bins = np.arange(1, FREQ + 1, dtype=np.int64)[None, :]
    angle = 2.0 * math.pi / LEN * (times * bins % LEN)
    real, imag = np.cos(angle), -np.sin(angle)
    pieces = [
        np.concatenate([real[:, p * WIDE : (p + 1) * WIDE], imag[:, p * WIDE : (p + 1) * WIDE]], 1)
        for p in range(PIECES)
    ]
    return np.stack(pieces).astype(np.float32).astype(BF16)


def inverse_matrix():
    bins = np.arange(1, FREQ + 1, dtype=np.int64)[:, None]
    shifts = np.arange(LAGS, dtype=np.int64)[None, :] - LAGS // 2
    angle = 2.0 * math.pi / LEN * (bins * shifts % LEN)
    whole = np.concatenate([np.cos(angle), -np.sin(angle)], 0).astype(np.float32)
    high = whole.astype(BF16)
    low = (whole - high.astype(np.float32)).astype(BF16)
    return np.concatenate([high, low], 1)


def gather_rows(tiles, sub):
    for shift in (1, 2, 4):
        mask = (sub & shift) == 0
        tiles = [
            jnp.where(mask, a, b) + pltpu.roll(jnp.where(mask, b, a), 8 - shift, 0)
            for a, b in zip(tiles[::2], tiles[1::2])
        ]
    return tiles[0]


def kernel(
    scale, rec_hbm, fwd_hbm, inv_hbm, out_ref,
    rec, fwd, inv, own, held, down, up, cross, lag, from_row, from_next,
    rec_sem, fwd_sem, inv_sem, xs_sem, xr_sem, ys_sem, yr_sem, os_sem, or_sem,
):
    chan, tm = lax.axis_index("chan"), lax.axis_index("tm")
    x, row = lax.rem(chan, ROW), chan // ROW
    rows = lax.axis_size("chan") // ROW
    row_before, row_after = lax.rem(row + rows - 1, rows), lax.rem(row + 1, rows)

    def fwd_copy(p):
        return pltpu.make_async_copy(fwd_hbm.at[p], fwd.at[p], fwd_sem.at[p])

    def rec_copy(k):
        return pltpu.make_async_copy(rec_hbm.at[:, pl.ds(4 * k, 4)], rec.at[k], rec_sem.at[k])

    rec_copy(0).start()
    for p in range(PIECES):
        fwd_copy(p).start()
    inv_copy = pltpu.make_async_copy(inv_hbm, inv, inv_sem)
    inv_copy.start()

    @pl.loop(1, CHUNKS)
    def _(k):
        rec_copy(k).start()

    barrier = pltpu.get_barrier_semaphore()

    def greet(there):
        pl.semaphore_signal(barrier, inc=1, device_id=there, device_id_type=MESH)

    for d in range(1, ROW):
        greet((row * ROW + lax.rem(x + d, ROW), tm))
    greet((row_before * ROW + x, tm))
    greet((row_after * ROW + x, tm))
    for t in range(TM):

        @pl.when(jnp.logical_or(x != tm, tm != t))
        def _():
            greet((row * ROW + tm, t))

        greet((row_after * ROW + tm, t))
    peers = ROW - 1 + 2 + TM + TM

    @pl.when(x != tm)
    def _():
        pl.semaphore_wait(barrier, peers)

    @pl.when(x == tm)
    def _():
        pl.semaphore_wait(barrier, peers - 1)

    def x_send(k, d):
        there = lax.rem(x + d, ROW)
        return pltpu.make_async_remote_copy(
            src_ref=own.at[there, k], dst_ref=held.at[k, :, x],
            send_sem=xs_sem.at[k, d - 1], recv_sem=xr_sem.at[k, d - 1],
            device_id=(row * ROW + there, tm), device_id_type=MESH,
        )

    def down_send(k):
        return pltpu.make_async_remote_copy(
            src_ref=held.at[k, 0], dst_ref=down.at[k],
            send_sem=ys_sem.at[k, 0], recv_sem=yr_sem.at[k, 0],
            device_id=(row_before * ROW + x, tm), device_id_type=MESH,
        )

    def up_send(k):
        return pltpu.make_async_remote_copy(
            src_ref=held.at[k, 1], dst_ref=up.at[k],
            send_sem=ys_sem.at[k, 1], recv_sem=yr_sem.at[k, 1],
            device_id=(row_after * ROW + x, tm), device_id_type=MESH,
        )

    def row_result(i):
        return pltpu.make_async_remote_copy(
            src_ref=lag.at[i], dst_ref=from_row.at[tm],
            send_sem=os_sem.at[i, 0], recv_sem=or_sem.at[tm, 0],
            device_id=(row * ROW + i, x), device_id_type=MESH,
        )

    def next_result(i):
        return pltpu.make_async_remote_copy(
            src_ref=lag.at[i, 1], dst_ref=from_next.at[tm],
            send_sem=os_sem.at[i, 1], recv_sem=or_sem.at[tm, 1],
            device_id=(row_before * ROW + i, x), device_id_type=MESH,
        )

    def whiten(k):
        rec_copy(k).wait()
        data = rec[k].reshape(128, LEN)
        reals, imags, mags = [], [], []
        for p in range(PIECES):

            @pl.when(k == 0)
            def _():
                fwd_copy(p).wait()

            spectrum = jnp.dot(data, fwd[p], preferred_element_type=F32)
            real, imag = spectrum[:, :WIDE], spectrum[:, WIDE:]
            reals.append(real)
            imags.append(imag)
            mags.append(jnp.sqrt(real * real + imag * imag))
        total = sum(jnp.sum(mag, axis=1, keepdims=True) for mag in mags)
        floor = 0.1 * (total * (1.0 / FREQ)) + 1e-06
        for p in range(PIECES):
            inverse = 1.0 / (mags[p] + floor)
            for at, part in ((p * WIDE, reals[p]), (FREQ + p * WIDE, imags[p])):
                white = (part * inverse).astype(BF16).reshape(ROW, 2, 16, WIDE)
                for there in range(ROW):
                    own[there, k, :, :, at : at + WIDE] = white[there]
        held[k, :, x] = own[x, k]

    sub = lax.broadcasted_iota(jnp.int32, (8, 128), 0)

    def correlate(k):
        @pl.loop(0, FREQ // 128)
        def _(tile):
            real_at = pl.ds(pl.multiple_of(tile * 128, 128), 128)
            imag_at = pl.ds(pl.multiple_of(FREQ + tile * 128, 128), 128)

            def load(ref, *at):
                real = ref[*at, :, real_at].astype(F32)
                imag = ref[*at, :, imag_at].astype(F32)
                return [(real[c * 8 : c * 8 + 8], imag[c * 8 : c * 8 + 8]) for c in range(2)]

            for half in range(2):
                here = [load(held, k, half, i) for i in range(ROW)]
                other = [load(down if half == 0 else up, k, i) for i in range(ROW)]
                for i in range(ROW):
                    real_tiles, imag_tiles = [], []
                    for offset in range(1, REACH + 1):
                        q = i + offset
                        if q < ROW:
                            left, right = here[i], here[q]
                        elif half == 0:
                            left, right = here[i], other[q - ROW]
                        else:
                            left, right = other[i], here[q - ROW]
                        for (ar, ai), (pr, pi) in zip(left, right):
                            real_tiles.append(ar * pr + ai * pi)
                            imag_tiles.append(ai * pr - ar * pi)
                    at = pl.ds((half * ROW + i) * 8, 8)
                    cross[at, real_at] = gather_rows(real_tiles, sub)
                    cross[at, imag_at] = gather_rows(imag_tiles, sub)

        whole = cross[...]
        high = whole.astype(BF16)
        low = (whole - high.astype(F32)).astype(BF16)
        first = jnp.dot(high, inv[...], preferred_element_type=F32)
        second = jnp.dot(low, inv[:, :LAGS], preferred_element_type=F32)
        lagged = (first[:, :LAGS] + (first[:, LAGS:] + second)) * scale
        for half in range(2):
            for i in range(ROW):
                at = (half * ROW + i) * 8
                lag[i, half, k] = lagged[at : at + 8]

    inv_copy.wait()

    @pl.loop(0, CHUNKS + 2)
    def _(step):
        @pl.when(step < CHUNKS)
        def _():
            whiten(step)
            for d in (2, 1, 3):
                x_send(step, d).start()

        @pl.when(jnp.logical_and(step >= 1, step < CHUNKS + 1))
        def _():
            k = step - 1
            for d in range(1, ROW):
                x_send(k, d).wait_recv()
            down_send(k).start()
            up_send(k).start()

        @pl.when(step >= 2)
        def _():
            k = step - 2
            down_send(k).wait_recv()
            up_send(k).wait_recv()
            correlate(k)

    for i in range(ROW):

        @pl.when(jnp.logical_or(x != tm, x != i))
        def _():
            row_result(i).start()

        @pl.when(jnp.logical_and(x == tm, x == i))
        def _():
            from_row[tm] = lag[i]

        next_result(i).start()

    @pl.loop(0, CHUNKS)
    def _(k):
        for d in range(1, ROW):
            x_send(k, d).wait_send()
        down_send(k).wait_send()
        up_send(k).wait_send()

    for i in range(ROW):

        @pl.when(jnp.logical_or(x != tm, x != i))
        def _():
            row_result(i).wait_send()

        next_result(i).wait_send()

    for t in range(TM):

        @pl.when(jnp.logical_or(x != tm, tm != t))
        def _():
            pltpu.make_async_remote_copy(
                src_ref=lag.at[0], dst_ref=from_row.at[t], send_sem=os_sem.at[0, 0],
                recv_sem=or_sem.at[t, 0], device_id=(row * ROW + tm, t), device_id_type=MESH,
            ).wait_recv()

        pltpu.make_async_remote_copy(
            src_ref=lag.at[0, 1], dst_ref=from_next.at[t], send_sem=os_sem.at[0, 1],
            recv_sem=or_sem.at[t, 1], device_id=(row_after * ROW + tm, t), device_id_type=MESH,
        ).wait_recv()

    inside = sub // 2 + 1 <= ROW - 1 - x
    for k in range(CHUNKS):
        out_ref[0, k] = (from_row[0, 0, k] + from_row[1, 0, k]) + (
            from_row[2, 0, k] + from_row[3, 0, k]
        )
        within = (from_row[0, 1, k] + from_row[1, 1, k]) + (
            from_row[2, 1, k] + from_row[3, 1, k]
        )
        across = (from_next[0, k] + from_next[1, k]) + (from_next[2, k] + from_next[3, k])
        out_ref[1, k] = jnp.where(inside, within, across)


def body(records, partners):
    channels, windows, length = records.shape
    total_windows = windows * lax.axis_size("tm")
    scale = 1.0 / math.sqrt(total_windows * FREQ)
    dma = pltpu.SemaphoreType.DMA
    result = pl.pallas_call(
        functools.partial(kernel, scale),
        out_shape=jax.ShapeDtypeStruct((2, CHUNKS, 8, LAGS), F32),
        in_specs=[pl.BlockSpec(memory_space=pl.ANY)] * 3,
        out_specs=pl.BlockSpec(memory_space=pltpu.VMEM),
        scratch_shapes=[
            pltpu.VMEM((CHUNKS, ROW, 4, windows, length), BF16),
            pltpu.VMEM((PIECES, LEN, 2 * WIDE), BF16),
            pltpu.VMEM((2 * FREQ, 2 * LAGS), BF16),
            pltpu.VMEM((ROW, CHUNKS, 2, 16, 2 * FREQ), BF16),
            pltpu.VMEM((CHUNKS, 2, ROW, 16, 2 * FREQ), BF16),
            pltpu.VMEM((CHUNKS, ROW, 16, 2 * FREQ), BF16),
            pltpu.VMEM((CHUNKS, ROW, 16, 2 * FREQ), BF16),
            pltpu.VMEM((64, 2 * FREQ), F32),
            pltpu.VMEM((ROW, 2, CHUNKS, 8, LAGS), F32),
            pltpu.VMEM((TM, 2, CHUNKS, 8, LAGS), F32),
            pltpu.VMEM((TM, CHUNKS, 8, LAGS), F32),
            dma((CHUNKS,)), dma((PIECES,)), dma,
            dma((CHUNKS, 3)), dma((CHUNKS, 3)),
            dma((CHUNKS, 2)), dma((CHUNKS, 2)),
            dma((ROW, 2)), dma((TM, 2)),
        ],
        compiler_params=pltpu.CompilerParams(
            collective_id=0, has_side_effects=True, vmem_limit_bytes=56 << 20
        ),
        cost_estimate=pl.CostEstimate(
            flops=7 * 10**9, bytes_accessed=12 * 10**6, transcendentals=10**6
        ),
    )(
        records.reshape(ROW, channels // ROW, windows, length),
        jnp.asarray(forward_matrix()),
        jnp.asarray(inverse_matrix()),
    )
    result = result.reshape(2, CHUNKS, REACH, 2, LAGS)
    lagged = result.transpose(2, 1, 0, 3, 4).reshape(REACH, channels // TM, LAGS)
    offsets = partners[0] - lax.axis_index("chan")
    chosen = 0.0
    for k in range(REACH):
        chosen = chosen + jnp.where((offsets == k + 1)[:, None, None], lagged[k][None], 0.0)
    return chosen[None]


def solution(mesh):
    return jax.shard_map(
        body,
        mesh=mesh,
        in_specs=(P("chan", "tm", None), P("chan", None)),
        out_specs=P("chan", None, "tm", None),
        check_vma=False,
    )
```

```python
import functools
import math

import jax
import jax.numpy as jnp
import numpy as np
from jax import lax
from jax.experimental import pallas as pl
from jax.experimental.pallas import tpu as pltpu
from jax.sharding import PartitionSpec as P

FREQ = 768
LAGS = 128
REACH = 4
LEN = 1920
ROW = 4
TM = 4
CHUNKS = 4
PIECES = 3
UNITS = CHUNKS * PIECES
PASS, USE = 1, 4
WIDE = FREQ // PIECES
MESH = pl.DeviceIdType.MESH
F32 = jnp.float32
BF16 = jnp.bfloat16
RESULT = jnp.bfloat16


def forward_matrix():
    times = np.arange(LEN, dtype=np.int64)[:, None]
    bins = np.arange(1, FREQ + 1, dtype=np.int64)[None, :]
    angle = 2.0 * math.pi / LEN * (times * bins % LEN)
    real, imag = np.cos(angle), -np.sin(angle)
    pieces = [
        np.concatenate([real[:, p * WIDE : (p + 1) * WIDE], imag[:, p * WIDE : (p + 1) * WIDE]], 1)
        for p in range(PIECES)
    ]
    return np.stack(pieces).astype(np.float32).astype(BF16)


def inverse_matrix():
    bins = np.arange(1, FREQ + 1, dtype=np.int64)[:, None]
    shifts = np.arange(LAGS, dtype=np.int64)[None, :] - LAGS // 2
    angle = 2.0 * math.pi / LEN * (bins * shifts % LEN)
    whole = np.concatenate([np.cos(angle), -np.sin(angle)], 0).astype(np.float32)
    high = whole.astype(BF16)
    low = (whole - high.astype(np.float32)).astype(BF16)
    both = np.concatenate([high, low], 1).reshape(2, PIECES, WIDE, 2 * LAGS)
    return both.transpose(1, 0, 2, 3).reshape(PIECES, 2 * WIDE, 2 * LAGS)


def gather_rows(tiles, sub):
    for shift in (1, 2, 4):
        mask = (sub & shift) == 0
        tiles = [
            jnp.where(mask, a, b) + pltpu.roll(jnp.where(mask, b, a), 8 - shift, 0)
            for a, b in zip(tiles[::2], tiles[1::2])
        ]
    return tiles[0]


def kernel(
    scale, rec_hbm, fwd_hbm, inv_hbm, out_ref,
    rec, fwd, inv, own, held, down, up, relay, cross, total, mine, mates, lag, from_row, from_next,
    rec_sem, fwd_sem, inv_sem, xs_sem, xr_sem, ys_sem, yr_sem, rs_sem, rr_sem, ms_sem, mr_sem, os_sem, or_sem,
):
    chan, tm = lax.axis_index("chan"), lax.axis_index("tm")
    rows = lax.axis_size("chan") // ROW
    planes = rows // ROW
    x, row = lax.rem(chan, ROW), chan // ROW
    y, plane = lax.rem(row, ROW), row // ROW
    has_before, has_after = row > 0, row < rows - 1
    core, pair = lax.rem(tm, 2), tm // 2
    mate = tm + 1 - 2 * core
    sums = lax.rem(x + tm, 2) == 0
    first, last = y == 0, y == ROW - 1
    passes_down = jnp.logical_and(last, plane > 0)
    passes_up = jnp.logical_and(first, plane < planes - 1)

    def device(by, at=x):
        return lax.rem(row + rows + by, rows) * ROW + at

    def fwd_copy(p):
        return pltpu.make_async_copy(fwd_hbm.at[p], fwd.at[p], fwd_sem.at[p])

    def rec_copy(c):
        return pltpu.make_async_copy(rec_hbm.at[:, c], rec.at[c], rec_sem.at[c])

    rec_copy(0).start()
    for p in range(PIECES):
        fwd_copy(p).start()
    inv_copy = pltpu.make_async_copy(inv_hbm, inv, inv_sem)
    inv_copy.start()
    for c in range(1, CHUNKS):
        rec_copy(c).start()

    from_next[...] = jnp.zeros(from_next.shape, from_next.dtype)
    barrier = pltpu.get_barrier_semaphore()

    def greet(*there):
        pl.semaphore_signal(barrier, inc=1, device_id=there, device_id_type=MESH)

    for d in range(1, ROW):
        greet(device(0, lax.rem(x + d, ROW)), tm)
    for t in range(TM // 2):

        @pl.when(jnp.logical_or(x != tm, pair != t))
        def _():
            greet(device(0, tm), 2 * t + core)

    @pl.when(sums)
    def _():
        greet(chan, mate)

    @pl.when(has_before)
    def _():
        greet(device(-1), tm)

        @pl.when(first)
        def _():
            greet(device(-ROW), tm)

    @pl.when(has_after)
    def _():
        greet(device(1), tm)
        for t in range(TM // 2):
            greet(device(1, tm), 2 * t + core)

        @pl.when(last)
        def _():
            greet(device(ROW), tm)

    @pl.when(passes_up)
    def _():
        greet(device(ROW - 1), tm)

    @pl.when(passes_down)
    def _():
        greet(device(1 - ROW), tm)

    itself = 1 - ((x - tm) * (x - tm) + 15) // 16
    before, after = (row + rows - 1) // rows, 1 - (row + 1) // rows
    edge = ((2 * y - 3) * (2 * y - 3)) // 9
    around = (plane + planes - 1) // planes + 1 - (plane + 1) // planes
    other = lax.rem(x + tm, 2)
    results = other + (1 - other) * (ROW - itself + ROW * before)
    peers = ROW - 1 + results + before + after + edge * around

    def x_send(u, half, d):
        c, p = u // PIECES, lax.rem(u, PIECES)
        there = lax.rem(x + d, ROW)
        return pltpu.make_async_remote_copy(
            src_ref=own.at[there, c, p, half], dst_ref=held.at[c, p, half, x],
            send_sem=xs_sem.at[u, half, d - 1], recv_sem=xr_sem.at[u, half, d - 1],
            device_id=(device(0, there), tm), device_id_type=MESH,
        )

    def straight(u, half, part):
        c, p = u // PIECES, lax.rem(u, PIECES)
        at = pl.ds(2 * part, 2)
        return pltpu.make_async_remote_copy(
            src_ref=held.at[c, p, half, at], dst_ref=(up if half else down).at[c, p, at],
            send_sem=ys_sem.at[u, half, part], recv_sem=yr_sem.at[u, half, part],
            device_id=(device(1 if half else -1), tm), device_id_type=MESH,
        )

    def detour(u, half):
        c, p = u // PIECES, lax.rem(u, PIECES)
        return pltpu.make_async_remote_copy(
            src_ref=held.at[c, p, half, pl.ds(2, 2)], dst_ref=relay.at[c, p],
            send_sem=ys_sem.at[u, half, 1], recv_sem=rr_sem.at[u],
            device_id=(device(1 - ROW if half else ROW - 1), tm), device_id_type=MESH,
        )

    def passed_on(u, half):
        c, p = u // PIECES, lax.rem(u, PIECES)
        return pltpu.make_async_remote_copy(
            src_ref=relay.at[c, p], dst_ref=(up if half else down).at[c, p, pl.ds(2, 2)],
            send_sem=rs_sem.at[u], recv_sem=yr_sem.at[u, half, 1],
            device_id=(device(ROW if half else -ROW), tm), device_id_type=MESH,
        )

    sends = ((0, has_before, first), (1, has_after, last))
    passes = ((0, passes_down), (1, passes_up))

    def halo_start(u):
        for half, wanted, at_edge in sends:

            @pl.when(jnp.logical_and(wanted, at_edge))
            def _():
                detour(u, half).start()

        for half, wanted, at_edge in sends:

            @pl.when(wanted)
            def _():
                straight(u, half, 0).start()

            @pl.when(jnp.logical_and(wanted, jnp.logical_not(at_edge)))
            def _():
                straight(u, half, 1).start()

    def pass_on(u):
        for half, wanted in passes:

            @pl.when(wanted)
            def _():
                detour(u, half).wait_recv()
                passed_on(u, half).start()

    def halo_arrived(u):
        for half, wanted in ((0, has_after), (1, has_before)):

            @pl.when(wanted)
            def _():
                for part in range(2):
                    straight(u, half, part).wait_recv()

    def halo_sent(u):
        for half, wanted, _ in sends:

            @pl.when(wanted)
            def _():
                for part in range(2):
                    straight(u, half, part).wait_send()

        for half, wanted in passes:

            @pl.when(wanted)
            def _():
                passed_on(u, half).wait_send()

    def mate_send(c):
        return pltpu.make_async_remote_copy(
            src_ref=mine.at[c], dst_ref=mates.at[c],
            send_sem=ms_sem.at[c], recv_sem=mr_sem.at[c],
            device_id=(chan, mate), device_id_type=MESH,
        )

    def row_result(c, i, t):
        return pltpu.make_async_remote_copy(
            src_ref=lag.at[i, c], dst_ref=from_row.at[t, c],
            send_sem=os_sem.at[i, c, 0], recv_sem=or_sem.at[t, c, 0],
            device_id=(device(0, i), x), device_id_type=MESH,
        )

    def next_result(c, i, t):
        at = pl.ds(16, 16) if i < 2 else pl.ds(0, 32)
        return pltpu.make_async_remote_copy(
            src_ref=lag.at[i, c, at], dst_ref=from_next.at[t, c, at],
            send_sem=os_sem.at[i, c, 1], recv_sem=or_sem.at[t, c, 1],
            device_id=(device(-1, i), x), device_id_type=MESH,
        )

    def whiten(c, half):
        @pl.when(half == 0)
        def _():
            rec_copy(c).wait()

        data = rec[c, :, half].reshape(128, LEN)
        reals, imags, mags = [], [], []
        for p in range(PIECES):
            if isinstance(c, int) and c == 0 and half == 0:
                fwd_copy(p).wait()
            spectrum = jnp.dot(data, fwd[p], preferred_element_type=F32)
            real, imag = spectrum[:, :WIDE], spectrum[:, WIDE:]
            reals.append(real)
            imags.append(imag)
            mags.append(jnp.sqrt(real * real + imag * imag))
        water = sum(jnp.sum(mag, axis=1, keepdims=True) for mag in mags) * (1.0 / FREQ)
        floor = 0.1 * water + 1e-06
        for p in range(PIECES):
            inverse = 1.0 / (mags[p] + floor)
            for at, part in ((0, reals[p]), (WIDE, imags[p])):
                white = (part * inverse).astype(BF16).reshape(ROW, 32, WIDE)
                for there in range(ROW):
                    own[there, c, p, half, :, at : at + WIDE] = white[there]
        for p in range(PIECES):
            held[c, p, half, x] = own[x, c, p, half]

    sub = lax.broadcasted_iota(jnp.int32, (8, 128), 0)

    def correlate(c, p):
        for lane in range(0, WIDE, 128):

            def load(ref, *at):
                both = []
                for lanes in (lane, WIDE + lane):
                    part = ref[*at, :, lanes : lanes + 128].astype(F32)
                    both.append([part[8 * n : 8 * n + 8] for n in range(4)])
                return list(zip(*both))

            here = [[load(held, c, p, half, i) for i in range(ROW)] for half in range(2)]
            after = [load(down, c, p, i) for i in range(ROW)]
            before = [load(up, c, p, i) for i in range(ROW)]
            for i in range(ROW):
                for offset in range(1, REACH + 1):
                    q = i + offset
                    if q < ROW:
                        lefts = here[0][i] + here[1][i]
                        rights = here[0][q] + here[1][q]
                    else:
                        lefts = here[0][i] + before[i]
                        rights = after[q - ROW] + here[1][q - ROW]
                    pairs = list(zip(lefts, rights))
                    reals = [ar * pr + ai * pi for (ar, ai), (pr, pi) in pairs]
                    imags = [ai * pr - ar * pi for (ar, ai), (pr, pi) in pairs]
                    at = (i * REACH + offset - 1) * 8
                    cross[at : at + 8, lane : lane + 128] = gather_rows(reals, sub)
                    cross[at : at + 8, WIDE + lane : WIDE + lane + 128] = gather_rows(imags, sub)

        whole = cross[...]
        high = whole.astype(BF16)
        low = (whole - high.astype(F32)).astype(BF16)
        first = jnp.dot(high, inv[p], preferred_element_type=F32)
        second = jnp.dot(low, inv[p, :, :LAGS], preferred_element_type=F32)
        term = first[:, :LAGS] + (first[:, LAGS:] + second)

        @pl.when(p == 0)
        def _():
            total[...] = term

        @pl.when(p > 0)
        def _():
            total[...] += term

    def keep_results(c):
        mine[c] = total[...] * scale

        @pl.when(jnp.logical_not(sums))
        def _():
            mate_send(c).start()

    def send_results(c):
        @pl.when(sums)
        def _():
            mate_send(c).wait_recv()
            for i in range(ROW):
                at = pl.ds(32 * i, 32)
                lag[i, c] = (mine[c, at] + mates[c, at]).astype(lag.dtype)

                @pl.when(jnp.logical_or(x != tm, x != i))
                def _():
                    row_result(c, i, pair).start()

                @pl.when(jnp.logical_and(x == tm, x == i))
                def _():
                    from_row[pair, c] = lag[i, c]

                @pl.when(has_before)
                def _():
                    next_result(c, i, pair).start()

    def results_sent(c):
        @pl.when(sums)
        def _():
            for i in range(ROW):

                @pl.when(jnp.logical_or(x != tm, x != i))
                def _():
                    row_result(c, i, pair).wait_send()

                @pl.when(has_before)
                def _():
                    next_result(c, i, pair).wait_send()

        @pl.when(jnp.logical_not(sums))
        def _():
            mate_send(c).wait_send()

    @pl.when(jnp.logical_not(has_before))
    def _():
        @pl.loop(0, CHUNKS)
        def _(c):
            up[c] = jnp.zeros(up.shape[1:], up.dtype)

    @pl.when(jnp.logical_not(has_after))
    def _():
        @pl.loop(0, CHUNKS)
        def _(c):
            down[c] = jnp.zeros(down.shape[1:], down.dtype)

    def x_start(u, half):
        for d in (2, 1, 3):
            x_send(u, half, d).start()

    early = PIECES // 2 + 1
    whiten(0, 0)
    pl.semaphore_wait(barrier, peers)
    for u in range(early):
        x_start(u, 0)
    whiten(0, 1)
    for u in range(early):
        x_start(u, 1)
    for u in range(early, PIECES):
        for half in range(2):
            x_start(u, half)
    inv_copy.wait()

    @pl.loop(0, UNITS + USE)
    def _(u):
        @pl.when(u < UNITS)
        def _():
            for half in range(2):
                for d in range(1, ROW):
                    x_send(u, half, d).wait_recv()
            halo_start(u)

        ahead = u // PIECES + 1
        part = lax.rem(u, PIECES)

        @pl.when(jnp.logical_and(ahead < CHUNKS, part < 2))
        def _():
            whiten(ahead, part)

        @pl.when(jnp.logical_and(ahead < CHUNKS, part == 1))
        def _():
            for p in range(PIECES):
                for half in range(2):
                    x_start(ahead * PIECES + p, half)

        @pl.when(jnp.logical_and(u >= PASS, u < UNITS + PASS))
        def _():
            pass_on(u - PASS)

        @pl.when(u >= USE)
        def _():
            k = u - USE
            c, p = k // PIECES, lax.rem(k, PIECES)
            halo_arrived(k)
            correlate(c, p)
            for half in range(2):
                for d in range(1, ROW):
                    x_send(k, half, d).wait_send()
            halo_sent(k)

            @pl.when(p == PIECES - 1)
            def _():
                keep_results(c)

            @pl.when(jnp.logical_and(p == 0, c > 0))
            def _():
                send_results(c - 1)

    send_results(CHUNKS - 1)
    for c in range(CHUNKS):
        for t in range(TM // 2):

            @pl.when(jnp.logical_or(x != tm, pair != t))
            def _():
                row_result(c, 0, t).wait_recv()

            @pl.when(jnp.logical_and(has_after, x < 2))
            def _():
                next_result(c, 0, t).wait_recv()

            @pl.when(jnp.logical_and(has_after, x >= 2))
            def _():
                next_result(c, 2, t).wait_recv()

        for offset in range(1, REACH + 1):
            within = jnp.logical_or(sub < 4, x + offset < ROW)
            at = pl.ds((offset - 1) * 8, 8)
            terms = [
                jnp.where(within, from_row[t, c, at].astype(F32), from_next[t, c, at].astype(F32))
                for t in range(TM // 2)
            ]
            out_ref[offset - 1, 8 * c : 8 * c + 8] = terms[0] + terms[1]
    for c in range(CHUNKS):
        results_sent(c)


def body(records, partners):
    channels, windows, length = records.shape
    total_windows = windows * lax.axis_size("tm")
    scale = 1.0 / math.sqrt(total_windows * FREQ)
    dma = pltpu.SemaphoreType.DMA
    lagged = pl.pallas_call(
        functools.partial(kernel, scale),
        out_shape=jax.ShapeDtypeStruct((REACH, channels // TM, LAGS), F32),
        in_specs=[pl.BlockSpec(memory_space=pl.ANY)] * 3,
        out_specs=pl.BlockSpec(memory_space=pltpu.VMEM),
        scratch_shapes=[
            pltpu.VMEM((CHUNKS, ROW, 2, 4, windows, length), BF16),
            pltpu.VMEM((PIECES, LEN, 2 * WIDE), BF16),
            pltpu.VMEM((PIECES, 2 * WIDE, 2 * LAGS), BF16),
            pltpu.VMEM((ROW, CHUNKS, PIECES, 2, 32, 2 * WIDE), BF16),
            pltpu.VMEM((CHUNKS, PIECES, 2, ROW, 32, 2 * WIDE), BF16),
            pltpu.VMEM((CHUNKS, PIECES, ROW, 32, 2 * WIDE), BF16),
            pltpu.VMEM((CHUNKS, PIECES, ROW, 32, 2 * WIDE), BF16),
            pltpu.VMEM((CHUNKS, PIECES, 2, 32, 2 * WIDE), BF16),
            pltpu.VMEM((128, 2 * WIDE), F32),
            pltpu.VMEM((128, LAGS), F32),
            pltpu.VMEM((CHUNKS, 128, LAGS), F32),
            pltpu.VMEM((CHUNKS, 128, LAGS), F32),
            pltpu.VMEM((ROW, CHUNKS, 32, LAGS), RESULT),
            pltpu.VMEM((TM // 2, CHUNKS, 32, LAGS), RESULT),
            pltpu.VMEM((TM // 2, CHUNKS, 32, LAGS), RESULT),
            dma((CHUNKS,)), dma((PIECES,)), dma,
            dma((UNITS, 2, 3)), dma((UNITS, 2, 3)),
            dma((UNITS, 2, 2)), dma((UNITS, 2, 2)),
            dma((UNITS,)), dma((UNITS,)),
            dma((CHUNKS,)), dma((CHUNKS,)),
            dma((ROW, CHUNKS, 2)), dma((TM // 2, CHUNKS, 2)),
        ],
        compiler_params=pltpu.CompilerParams(
            collective_id=0, has_side_effects=True, vmem_limit_bytes=56 << 20
        ),
        cost_estimate=pl.CostEstimate(
            flops=7 * 10**9, bytes_accessed=12 * 10**6, transcendentals=10**6
        ),
    )(
        records.reshape(ROW, CHUNKS, 2, channels // (ROW * CHUNKS * 2), windows, length),
        jnp.asarray(forward_matrix()),
        jnp.asarray(inverse_matrix()),
    )
    offsets = partners[0] - lax.axis_index("chan")
    chosen = 0.0
    for k in range(REACH):
        chosen = chosen + jnp.where((offsets == k + 1)[:, None, None], lagged[k][None], 0.0)
    return chosen[None]


def solution(mesh):
    return jax.shard_map(
        body,
        mesh=mesh,
        in_specs=(P("chan", "tm", None), P("chan", None)),
        out_specs=P("chan", None, "tm", None),
        check_vma=False,
    )
```

```python
import functools
import math

import jax
import jax.numpy as jnp
import numpy as np
from jax import lax
from jax.experimental import pallas as pl
from jax.experimental.pallas import tpu as pltpu
from jax.sharding import PartitionSpec as P

FREQ = 768
LAGS = 128
REACH = 4
LEN = 1920
ROW = 4
TM = 4
CHUNKS = 4
PIECES = 3
UNITS = CHUNKS * PIECES
PASS, USE = 2, 5
WIDE = FREQ // PIECES
MESH = pl.DeviceIdType.MESH
F32 = jnp.float32
BF16 = jnp.bfloat16
RESULT = jnp.bfloat16


def forward_matrix():
    times = np.arange(LEN, dtype=np.int64)[:, None]
    bins = np.arange(1, FREQ + 1, dtype=np.int64)[None, :]
    angle = 2.0 * math.pi / LEN * (times * bins % LEN)
    real, imag = np.cos(angle), -np.sin(angle)
    pieces = [
        np.concatenate([real[:, p * WIDE : (p + 1) * WIDE], imag[:, p * WIDE : (p + 1) * WIDE]], 1)
        for p in range(PIECES)
    ]
    return np.stack(pieces).astype(np.float32).astype(BF16)


def inverse_matrix():
    bins = np.arange(1, FREQ + 1, dtype=np.int64)[:, None]
    shifts = np.arange(LAGS, dtype=np.int64)[None, :] - LAGS // 2
    angle = 2.0 * math.pi / LEN * (bins * shifts % LEN)
    whole = np.concatenate([np.cos(angle), -np.sin(angle)], 0).astype(np.float32)
    high = whole.astype(BF16)
    low = (whole - high.astype(np.float32)).astype(BF16)
    both = np.concatenate([high, low], 1).reshape(2, PIECES, WIDE, 2 * LAGS)
    return both.transpose(1, 0, 2, 3).reshape(PIECES, 2 * WIDE, 2 * LAGS)


def gather_rows(tiles, sub):
    for shift in (1, 2, 4):
        mask = (sub & shift) == 0
        tiles = [
            jnp.where(mask, a, b) + pltpu.roll(jnp.where(mask, b, a), 8 - shift, 0)
            for a, b in zip(tiles[::2], tiles[1::2])
        ]
    return tiles[0]


def kernel(
    scale, rec_hbm, fwd_hbm, inv_hbm, out_ref,
    rec, fwd, inv, own, held, down, up, relay, cross, total, mine, mates, lag, from_row, from_next,
    rec_sem, fwd_sem, inv_sem, xs_sem, xr_sem, ys_sem, yr_sem, rs_sem, rr_sem, ms_sem, mr_sem, os_sem, or_sem,
):
    chan, tm = lax.axis_index("chan"), lax.axis_index("tm")
    rows = lax.axis_size("chan") // ROW
    planes = rows // ROW
    x, row = lax.rem(chan, ROW), chan // ROW
    y, plane = lax.rem(row, ROW), row // ROW
    has_before, has_after = row > 0, row < rows - 1
    core, pair = lax.rem(tm, 2), tm // 2
    mate = tm + 1 - 2 * core
    sums = lax.rem(x + tm, 2) == 0
    first, last = y == 0, y == ROW - 1
    low, high = plane > 0, plane < planes - 1

    def device(by, at=x):
        return lax.rem(row + rows + by, rows) * ROW + at

    def fwd_copy(p):
        return pltpu.make_async_copy(fwd_hbm.at[p], fwd.at[p], fwd_sem.at[p])

    def rec_copy(c):
        return pltpu.make_async_copy(rec_hbm.at[:, c], rec.at[c], rec_sem.at[c])

    rec_copy(0).start()
    for p in range(PIECES):
        fwd_copy(p).start()
    inv_copy = pltpu.make_async_copy(inv_hbm, inv, inv_sem)
    inv_copy.start()
    for c in range(1, CHUNKS):
        rec_copy(c).start()

    from_next[...] = jnp.zeros(from_next.shape, from_next.dtype)
    barrier = pltpu.get_barrier_semaphore()

    def greet(*there):
        pl.semaphore_signal(barrier, inc=1, device_id=there, device_id_type=MESH)

    for d in range(1, ROW):
        greet(device(0, lax.rem(x + d, ROW)), tm)
    for t in range(TM // 2):

        @pl.when(jnp.logical_or(x != tm, pair != t))
        def _():
            greet(device(0, tm), 2 * t + core)

    @pl.when(sums)
    def _():
        greet(chan, mate)

    @pl.when(jnp.logical_not(first))
    def _():
        greet(device(-1), tm)

    @pl.when(jnp.logical_not(last))
    def _():
        greet(device(1), tm)

    @pl.when(has_after)
    def _():
        for t in range(TM // 2):
            greet(device(1, tm), 2 * t + core)

    for at_edge, near in ((first, ROW - 1), (last, 1 - ROW)):
        for there, far in ((low, -ROW), (high, ROW)):

            @pl.when(jnp.logical_and(at_edge, there))
            def _():
                greet(device(near), tm)
                greet(device(far), tm)

    itself = 1 - ((x - tm) * (x - tm) + 15) // 16
    before = (row + rows - 1) // rows
    edge = ((2 * y - 3) * (2 * y - 3)) // 9
    around = (plane + planes - 1) // planes + 1 - (plane + 1) // planes
    other = lax.rem(x + tm, 2)
    results = other + (1 - other) * (ROW - itself + ROW * before)
    peers = ROW - 1 + results + 2 - edge + 2 * edge * around

    def x_send(u, d, half=None):
        c, p = u // PIECES, lax.rem(u, PIECES)
        there = lax.rem(x + d, ROW)
        at = (c, p) if half is None else (c, p, half)
        to = held.at[c, p, :, x] if half is None else held.at[c, p, half, x]
        return pltpu.make_async_remote_copy(
            src_ref=own.at[there, *at], dst_ref=to, send_sem=xs_sem, recv_sem=xr_sem.at[u],
            device_id=(device(0, there), tm), device_id_type=MESH,
        )

    def x_arrived(u):
        part = held.at[u // PIECES, lax.rem(u, PIECES), :, pl.ds(0, ROW - 1)]
        pltpu.make_async_remote_copy(
            src_ref=part, dst_ref=part, send_sem=xs_sem, recv_sem=xr_sem.at[u],
            device_id=(device(0, lax.rem(x + 1, ROW)), tm), device_id_type=MESH,
        ).wait_recv()

    def x_sent():
        part = own.at[pl.ds(0, ROW - 1)]
        pltpu.make_async_remote_copy(
            src_ref=part, dst_ref=part, send_sem=xs_sem, recv_sem=xr_sem.at[0],
            device_id=(device(0, lax.rem(x + 1, ROW)), tm), device_id_type=MESH,
        ).wait_send()

    def straight(u, half):
        c, p = u // PIECES, lax.rem(u, PIECES)
        return pltpu.make_async_remote_copy(
            src_ref=held.at[c, p, half], dst_ref=(up if half else down).at[c, p],
            send_sem=ys_sem.at[half], recv_sem=yr_sem.at[u, half],
            device_id=(device(1 if half else -1), tm), device_id_type=MESH,
        )

    def cross_y(u, half):
        c, p = u // PIECES, lax.rem(u, PIECES)
        return pltpu.make_async_remote_copy(
            src_ref=held.at[c, p, half, pl.ds(2, 2)], dst_ref=relay.at[1, c, p],
            send_sem=ys_sem.at[half], recv_sem=rr_sem.at[u, 1],
            device_id=(device(1 - ROW if half else ROW - 1), tm), device_id_type=MESH,
        )

    def cross_z(u, half):
        c, p = u // PIECES, lax.rem(u, PIECES)
        return pltpu.make_async_remote_copy(
            src_ref=held.at[c, p, half, pl.ds(0, 2)], dst_ref=relay.at[0, c, p],
            send_sem=ys_sem.at[half], recv_sem=rr_sem.at[u, 0],
            device_id=(device(ROW if half else -ROW), tm), device_id_type=MESH,
        )

    def then_z(u, half):
        c, p = u // PIECES, lax.rem(u, PIECES)
        return pltpu.make_async_remote_copy(
            src_ref=relay.at[1, c, p], dst_ref=(up if half else down).at[c, p, pl.ds(2, 2)],
            send_sem=rs_sem.at[1], recv_sem=yr_sem.at[u, half],
            device_id=(device(ROW if half else -ROW), tm), device_id_type=MESH,
        )

    def then_y(u, half):
        c, p = u // PIECES, lax.rem(u, PIECES)
        return pltpu.make_async_remote_copy(
            src_ref=relay.at[0, c, p], dst_ref=(up if half else down).at[c, p, pl.ds(0, 2)],
            send_sem=rs_sem.at[0], recv_sem=yr_sem.at[u, half],
            device_id=(device(1 - ROW if half else ROW - 1), tm), device_id_type=MESH,
        )

    down_here, up_here = jnp.logical_not(first), jnp.logical_not(last)
    inner = ((0, down_here), (1, up_here))
    edges = ((0, jnp.logical_and(first, low)), (1, jnp.logical_and(last, high)))
    turns_z = ((0, jnp.logical_and(last, low)), (1, jnp.logical_and(first, high)))
    turns_y = ((0, jnp.logical_and(first, high)), (1, jnp.logical_and(last, low)))

    def halo_start(u):
        for half, wanted in edges:

            @pl.when(wanted)
            def _():
                cross_z(u, half).start()
                cross_y(u, half).start()

        for half, wanted in inner:

            @pl.when(wanted)
            def _():
                straight(u, half).start()

    def pass_on(u):
        for half, wanted in turns_z:

            @pl.when(wanted)
            def _():
                cross_y(u, half).wait_recv()
                then_z(u, half).start()

        for half, wanted in turns_y:

            @pl.when(wanted)
            def _():
                cross_z(u, half).wait_recv()
                then_y(u, half).start()

    def halo_arrived(u):
        for half, wanted in ((0, has_after), (1, has_before)):

            @pl.when(wanted)
            def _():
                straight(u, half).wait_recv()

    def halo_sent():
        for half, wanted in ((0, has_before), (1, has_after)):
            whole = up if half else down

            @pl.when(wanted)
            def _():
                pltpu.make_async_remote_copy(
                    src_ref=whole, dst_ref=whole, send_sem=ys_sem.at[half],
                    recv_sem=yr_sem.at[0, half],
                    device_id=(device(1 if half else -1), tm), device_id_type=MESH,
                ).wait_send()

        for part, turns in ((1, turns_z), (0, turns_y)):
            for half, wanted in turns:
                whole = relay.at[part]

                @pl.when(wanted)
                def _():
                    pltpu.make_async_remote_copy(
                        src_ref=whole, dst_ref=whole, send_sem=rs_sem.at[part],
                        recv_sem=yr_sem.at[0, half],
                        device_id=(device(1 if half else -1), tm), device_id_type=MESH,
                    ).wait_send()

    def mate_send(c):
        return pltpu.make_async_remote_copy(
            src_ref=mine.at[c], dst_ref=mates.at[c],
            send_sem=ms_sem.at[c], recv_sem=mr_sem.at[c],
            device_id=(chan, mate), device_id_type=MESH,
        )

    def row_result(c, i, t):
        return pltpu.make_async_remote_copy(
            src_ref=lag.at[i, c], dst_ref=from_row.at[t, c],
            send_sem=os_sem.at[c, 0], recv_sem=or_sem.at[c, 0],
            device_id=(device(0, i), x), device_id_type=MESH,
        )

    def next_result(c, i, t):
        at = pl.ds(16, 16) if i < 2 else pl.ds(0, 32)
        return pltpu.make_async_remote_copy(
            src_ref=lag.at[i, c, at], dst_ref=from_next.at[t, c, at],
            send_sem=os_sem.at[c, 1], recv_sem=or_sem.at[c, 1],
            device_id=(device(-1, i), x), device_id_type=MESH,
        )

    def whiten(c, half):
        @pl.when(half == 0)
        def _():
            rec_copy(c).wait()

        data = rec[c, :, half].reshape(128, LEN)
        reals, imags, mags = [], [], []
        for p in range(PIECES):
            if isinstance(c, int) and c == 0 and half == 0:
                fwd_copy(p).wait()
            spectrum = jnp.dot(data, fwd[p], preferred_element_type=F32)
            real, imag = spectrum[:, :WIDE], spectrum[:, WIDE:]
            reals.append(real)
            imags.append(imag)
            mags.append(jnp.sqrt(real * real + imag * imag))
        water = sum(jnp.sum(mag, axis=1, keepdims=True) for mag in mags) * (1.0 / FREQ)
        floor = 0.1 * water + 1e-06
        for p in range(PIECES):
            inverse = 1.0 / (mags[p] + floor)
            for at, part in ((0, reals[p]), (WIDE, imags[p])):
                white = (part * inverse).astype(BF16).reshape(ROW, 32, WIDE)
                for there in range(ROW):
                    own[there, c, p, half, :, at : at + WIDE] = white[there]
        for p in range(PIECES):
            held[c, p, half, x] = own[x, c, p, half]

    sub = lax.broadcasted_iota(jnp.int32, (8, 128), 0)

    def correlate(c, p):
        for lane in range(0, WIDE, 128):

            def load(ref, *at):
                both = []
                for lanes in (lane, WIDE + lane):
                    part = ref[*at, :, lanes : lanes + 128].astype(F32)
                    both.append([part[8 * n : 8 * n + 8] for n in range(4)])
                return list(zip(*both))

            here = [[load(held, c, p, half, i) for i in range(ROW)] for half in range(2)]
            after = [load(down, c, p, i) for i in range(ROW)]
            before = [load(up, c, p, i) for i in range(ROW)]
            for i in range(ROW):
                for offset in range(1, REACH + 1):
                    q = i + offset
                    if q < ROW:
                        lefts = here[0][i] + here[1][i]
                        rights = here[0][q] + here[1][q]
                    else:
                        lefts = here[0][i] + before[i]
                        rights = after[q - ROW] + here[1][q - ROW]
                    pairs = list(zip(lefts, rights))
                    reals = [ar * pr + ai * pi for (ar, ai), (pr, pi) in pairs]
                    imags = [ai * pr - ar * pi for (ar, ai), (pr, pi) in pairs]
                    at = (i * REACH + offset - 1) * 8
                    cross[at : at + 8, lane : lane + 128] = gather_rows(reals, sub)
                    cross[at : at + 8, WIDE + lane : WIDE + lane + 128] = gather_rows(imags, sub)

        whole = cross[...]
        high = whole.astype(BF16)
        low = (whole - high.astype(F32)).astype(BF16)
        first = jnp.dot(high, inv[p], preferred_element_type=F32)
        second = jnp.dot(low, inv[p, :, :LAGS], preferred_element_type=F32)
        term = first[:, :LAGS] + (first[:, LAGS:] + second)

        @pl.when(p == 0)
        def _():
            total[...] = term

        @pl.when(p > 0)
        def _():
            total[...] += term

    def keep_results(c):
        mine[c] = total[...] * scale

        @pl.when(jnp.logical_not(sums))
        def _():
            mate_send(c).start()

    def send_results(c):
        @pl.when(sums)
        def _():
            mate_send(c).wait_recv()
            for i in range(ROW):
                at = pl.ds(32 * i, 32)
                lag[i, c] = (mine[c, at] + mates[c, at]).astype(lag.dtype)

                @pl.when(jnp.logical_or(x != tm, x != i))
                def _():
                    row_result(c, i, pair).start()

                @pl.when(jnp.logical_and(x == tm, x == i))
                def _():
                    from_row[pair, c] = lag[i, c]

                @pl.when(has_before)
                def _():
                    next_result(c, i, pair).start()

    def results_wait(c, kind, part):
        return pltpu.make_async_remote_copy(
            src_ref=part, dst_ref=part, send_sem=os_sem.at[c, kind], recv_sem=or_sem.at[c, kind],
            device_id=(device(-1 if kind else 0, x), x), device_id_type=MESH,
        )

    def results_sent(c):
        @pl.when(sums)
        def _():
            @pl.when(x != tm)
            def _():
                results_wait(c, 0, lag.at[:, c]).wait_send()

            @pl.when(x == tm)
            def _():
                results_wait(c, 0, lag.at[pl.ds(0, ROW - 1), c]).wait_send()

            @pl.when(has_before)
            def _():
                results_wait(c, 1, lag.at[pl.ds(0, ROW - 1), c]).wait_send()

        @pl.when(jnp.logical_not(sums))
        def _():
            mate_send(c).wait_send()

    def results_arrived(c):
        @pl.when(x != tm)
        def _():
            results_wait(c, 0, from_row.at[:, c]).wait_recv()

        @pl.when(x == tm)
        def _():
            results_wait(c, 0, from_row.at[pl.ds(0, 1), c]).wait_recv()

        @pl.when(jnp.logical_and(has_after, x < 2))
        def _():
            results_wait(c, 1, from_next.at[:, c, pl.ds(16, 16)]).wait_recv()

        @pl.when(jnp.logical_and(has_after, x >= 2))
        def _():
            results_wait(c, 1, from_next.at[:, c]).wait_recv()

    @pl.when(jnp.logical_not(has_before))
    def _():
        @pl.loop(0, CHUNKS)
        def _(c):
            up[c] = jnp.zeros(up.shape[1:], up.dtype)

    @pl.when(jnp.logical_not(has_after))
    def _():
        @pl.loop(0, CHUNKS)
        def _(c):
            down[c] = jnp.zeros(down.shape[1:], down.dtype)

    def x_start(u, half=None):
        for d in (2, 1, 3):
            x_send(u, d, half).start()

    early = PIECES // 2 + 1
    whiten(0, 0)
    pl.semaphore_wait(barrier, peers)
    for u in range(early):
        x_start(u, 0)
    whiten(0, 1)
    for u in range(early):
        x_start(u, 1)
    for u in range(early, PIECES):
        x_start(u)
    inv_copy.wait()

    @pl.loop(0, UNITS + USE)
    def _(u):
        @pl.when(u < UNITS)
        def _():
            x_arrived(u)
            halo_start(u)

        ahead, part = u // 2 + 1, lax.rem(u, 2)

        @pl.when(ahead < CHUNKS)
        def _():
            whiten(ahead, part)

        @pl.when(jnp.logical_and(ahead < CHUNKS, part == 1))
        def _():
            for p in range(PIECES):
                x_start(ahead * PIECES + p)

        @pl.when(jnp.logical_and(u >= PASS, u < UNITS + PASS))
        def _():
            pass_on(u - PASS)

        @pl.when(u >= USE)
        def _():
            k = u - USE
            c, p = k // PIECES, lax.rem(k, PIECES)
            halo_arrived(k)
            correlate(c, p)

            @pl.when(p == PIECES - 1)
            def _():
                keep_results(c)

            @pl.when(jnp.logical_and(p == 0, c > 0))
            def _():
                send_results(c - 1)

    send_results(CHUNKS - 1)
    x_sent()
    halo_sent()
    for c in range(CHUNKS):
        results_arrived(c)
        for offset in range(1, REACH + 1):
            within = jnp.logical_or(sub < 4, x + offset < ROW)
            at = pl.ds((offset - 1) * 8, 8)
            terms = [
                jnp.where(within, from_row[t, c, at].astype(F32), from_next[t, c, at].astype(F32))
                for t in range(TM // 2)
            ]
            out_ref[offset - 1, 8 * c : 8 * c + 8] = terms[0] + terms[1]
    for c in range(CHUNKS):
        results_sent(c)


def body(records, partners):
    channels, windows, length = records.shape
    total_windows = windows * lax.axis_size("tm")
    scale = 1.0 / math.sqrt(total_windows * FREQ)
    dma = pltpu.SemaphoreType.DMA
    lagged = pl.pallas_call(
        functools.partial(kernel, scale),
        out_shape=jax.ShapeDtypeStruct((REACH, channels // TM, LAGS), F32),
        in_specs=[pl.BlockSpec(memory_space=pl.ANY)] * 3,
        out_specs=pl.BlockSpec(memory_space=pltpu.VMEM),
        scratch_shapes=[
            pltpu.VMEM((CHUNKS, ROW, 2, 4, windows, length), BF16),
            pltpu.VMEM((PIECES, LEN, 2 * WIDE), BF16),
            pltpu.VMEM((PIECES, 2 * WIDE, 2 * LAGS), BF16),
            pltpu.VMEM((ROW, CHUNKS, PIECES, 2, 32, 2 * WIDE), BF16),
            pltpu.VMEM((CHUNKS, PIECES, 2, ROW, 32, 2 * WIDE), BF16),
            pltpu.VMEM((CHUNKS, PIECES, ROW, 32, 2 * WIDE), BF16),
            pltpu.VMEM((CHUNKS, PIECES, ROW, 32, 2 * WIDE), BF16),
            pltpu.VMEM((2, CHUNKS, PIECES, 2, 32, 2 * WIDE), BF16),
            pltpu.VMEM((128, 2 * WIDE), F32),
            pltpu.VMEM((128, LAGS), F32),
            pltpu.VMEM((CHUNKS, 128, LAGS), F32),
            pltpu.VMEM((CHUNKS, 128, LAGS), F32),
            pltpu.VMEM((ROW, CHUNKS, 32, LAGS), RESULT),
            pltpu.VMEM((TM // 2, CHUNKS, 32, LAGS), RESULT),
            pltpu.VMEM((TM // 2, CHUNKS, 32, LAGS), RESULT),
            dma((CHUNKS,)), dma((PIECES,)), dma,
            dma, dma((UNITS,)),
            dma((2,)), dma((UNITS, 2)),
            dma((2,)), dma((UNITS, 2)),
            dma((CHUNKS,)), dma((CHUNKS,)),
            dma((CHUNKS, 2)), dma((CHUNKS, 2)),
        ],
        compiler_params=pltpu.CompilerParams(
            collective_id=0, has_side_effects=True, vmem_limit_bytes=56 << 20
        ),
        cost_estimate=pl.CostEstimate(
            flops=7 * 10**9, bytes_accessed=12 * 10**6, transcendentals=10**6
        ),
    )(
        records.reshape(ROW, CHUNKS, 2, channels // (ROW * CHUNKS * 2), windows, length),
        jnp.asarray(forward_matrix()),
        jnp.asarray(inverse_matrix()),
    )
    offsets = partners[0] - lax.axis_index("chan")
    chosen = 0.0
    for k in range(REACH):
        chosen = chosen + jnp.where((offsets == k + 1)[:, None, None], lagged[k][None], 0.0)
    return chosen[None]


def solution(mesh):
    return jax.shard_map(
        body,
        mesh=mesh,
        in_specs=(P("chan", "tm", None), P("chan", None)),
        out_specs=P("chan", None, "tm", None),
        check_vma=False,
    )
```

```python
import functools
import math

import jax
import jax.numpy as jnp
import numpy as np
from jax import lax
from jax.experimental import pallas as pl
from jax.experimental.pallas import tpu as pltpu
from jax.sharding import PartitionSpec as P

FREQ = 768
LAGS = 128
REACH = 4
LEN = 1920
ROW = 4
TM = 4
CHUNKS = 4
PIECES = 3
UNITS = CHUNKS * PIECES
PASS, USE = 2, 5
WIDE = FREQ // PIECES
MESH = pl.DeviceIdType.MESH
F32 = jnp.float32
BF16 = jnp.bfloat16
RESULT = jnp.bfloat16


def forward_matrix():
    times = np.arange(LEN, dtype=np.int64)[:, None]
    bins = np.arange(1, FREQ + 1, dtype=np.int64)[None, :]
    angle = 2.0 * math.pi / LEN * (times * bins % LEN)
    real, imag = np.cos(angle), -np.sin(angle)
    pieces = [
        np.concatenate([real[:, p * WIDE : (p + 1) * WIDE], imag[:, p * WIDE : (p + 1) * WIDE]], 1)
        for p in range(PIECES)
    ]
    return np.stack(pieces).astype(np.float32).astype(BF16)


def inverse_matrix():
    bins = np.arange(1, FREQ + 1, dtype=np.int64)[:, None]
    shifts = np.arange(LAGS, dtype=np.int64)[None, :] - LAGS // 2
    angle = 2.0 * math.pi / LEN * (bins * shifts % LEN)
    whole = np.concatenate([np.cos(angle), -np.sin(angle)], 0).astype(np.float32)
    high = whole.astype(BF16)
    low = (whole - high.astype(np.float32)).astype(BF16)
    both = np.concatenate([high, low], 1).reshape(2, PIECES, WIDE, 2 * LAGS)
    return both.transpose(1, 0, 2, 3).reshape(PIECES, 2 * WIDE, 2 * LAGS)


def gather_rows(tiles, sub):
    for shift in (1, 2, 4):
        mask = (sub & shift) == 0
        tiles = [
            jnp.where(mask, a, b) + pltpu.roll(jnp.where(mask, b, a), 8 - shift, 0)
            for a, b in zip(tiles[::2], tiles[1::2])
        ]
    return tiles[0]


def kernel(
    scale, rec_hbm, fwd_hbm, inv_hbm, out_ref,
    rec, fwd, inv, own, held, down, up, relay, cross, total, mine, mates, lag, from_row, from_next,
    rec_sem, fwd_sem, inv_sem, xs_sem, xr_sem, ys_sem, yr_sem, rs_sem, rr_sem, ms_sem, mr_sem, os_sem, or_sem,
):
    chan, tm = lax.axis_index("chan"), lax.axis_index("tm")
    rows = lax.axis_size("chan") // ROW
    planes = rows // ROW
    x, row = lax.rem(chan, ROW), chan // ROW
    y, plane = lax.rem(row, ROW), row // ROW
    has_before, has_after = row > 0, row < rows - 1
    core, pair = lax.rem(tm, 2), tm // 2
    mate = tm + 1 - 2 * core
    sums = lax.rem(x + tm, 2) == 0
    first, last = y == 0, y == ROW - 1
    low, high = plane > 0, plane < planes - 1

    def device(by, at=x):
        return lax.rem(row + rows + by, rows) * ROW + at

    def fwd_copy(p):
        return pltpu.make_async_copy(fwd_hbm.at[p], fwd.at[p], fwd_sem.at[p])

    def rec_copy(c):
        return pltpu.make_async_copy(rec_hbm.at[:, c], rec.at[c], rec_sem.at[c])

    rec_copy(0).start()
    for p in range(PIECES):
        fwd_copy(p).start()
    inv_copy = pltpu.make_async_copy(inv_hbm, inv, inv_sem)

    from_next[...] = jnp.zeros(from_next.shape, from_next.dtype)
    barrier = pltpu.get_barrier_semaphore()

    def greet(*there):
        pl.semaphore_signal(barrier, inc=1, device_id=there, device_id_type=MESH)

    for d in range(1, ROW):
        greet(device(0, lax.rem(x + d, ROW)), tm)
    for t in range(TM // 2):

        @pl.when(jnp.logical_or(x != tm, pair != t))
        def _():
            greet(device(0, tm), 2 * t + core)

    @pl.when(sums)
    def _():
        greet(chan, mate)

    @pl.when(jnp.logical_not(first))
    def _():
        greet(device(-1), tm)

    @pl.when(jnp.logical_not(last))
    def _():
        greet(device(1), tm)

    @pl.when(has_after)
    def _():
        for t in range(TM // 2):
            greet(device(1, tm), 2 * t + core)

    for at_edge, near in ((first, ROW - 1), (last, 1 - ROW)):
        for there, far in ((low, -ROW), (high, ROW)):

            @pl.when(jnp.logical_and(at_edge, there))
            def _():
                greet(device(near), tm)
                greet(device(far), tm)

    itself = 1 - ((x - tm) * (x - tm) + 15) // 16
    before = (row + rows - 1) // rows
    edge = ((2 * y - 3) * (2 * y - 3)) // 9
    around = (plane + planes - 1) // planes + 1 - (plane + 1) // planes
    other = lax.rem(x + tm, 2)
    results = other + (1 - other) * (ROW - itself + ROW * before)
    peers = ROW - 1 + results + 2 - edge + 2 * edge * around

    def x_send(u, d, half=None):
        c, p = u // PIECES, lax.rem(u, PIECES)
        there = lax.rem(x + d, ROW)
        at = (c, p) if half is None else (c, p, half)
        to = held.at[c, p, :, x] if half is None else held.at[c, p, half, x]
        return pltpu.make_async_remote_copy(
            src_ref=own.at[there, *at], dst_ref=to, send_sem=xs_sem, recv_sem=xr_sem.at[u],
            device_id=(device(0, there), tm), device_id_type=MESH,
        )

    def x_arrived(u):
        part = held.at[u // PIECES, lax.rem(u, PIECES), :, pl.ds(0, ROW - 1)]
        pltpu.make_async_remote_copy(
            src_ref=part, dst_ref=part, send_sem=xs_sem, recv_sem=xr_sem.at[u],
            device_id=(device(0, lax.rem(x + 1, ROW)), tm), device_id_type=MESH,
        ).wait_recv()

    def x_sent():
        part = own.at[pl.ds(0, ROW - 1)]
        pltpu.make_async_remote_copy(
            src_ref=part, dst_ref=part, send_sem=xs_sem, recv_sem=xr_sem.at[0],
            device_id=(device(0, lax.rem(x + 1, ROW)), tm), device_id_type=MESH,
        ).wait_send()

    def straight(u, half):
        c, p = u // PIECES, lax.rem(u, PIECES)
        return pltpu.make_async_remote_copy(
            src_ref=held.at[c, p, half], dst_ref=(up if half else down).at[c, p],
            send_sem=ys_sem.at[half], recv_sem=yr_sem.at[u, half],
            device_id=(device(1 if half else -1), tm), device_id_type=MESH,
        )

    def cross_y(u, half):
        c, p = u // PIECES, lax.rem(u, PIECES)
        return pltpu.make_async_remote_copy(
            src_ref=held.at[c, p, half, pl.ds(2, 2)], dst_ref=relay.at[1, c, p],
            send_sem=ys_sem.at[half], recv_sem=rr_sem.at[u, 1],
            device_id=(device(1 - ROW if half else ROW - 1), tm), device_id_type=MESH,
        )

    def cross_z(u, half):
        c, p = u // PIECES, lax.rem(u, PIECES)
        return pltpu.make_async_remote_copy(
            src_ref=held.at[c, p, half, pl.ds(0, 2)], dst_ref=relay.at[0, c, p],
            send_sem=ys_sem.at[half], recv_sem=rr_sem.at[u, 0],
            device_id=(device(ROW if half else -ROW), tm), device_id_type=MESH,
        )

    def then_z(u, half):
        c, p = u // PIECES, lax.rem(u, PIECES)
        return pltpu.make_async_remote_copy(
            src_ref=relay.at[1, c, p], dst_ref=(up if half else down).at[c, p, pl.ds(2, 2)],
            send_sem=rs_sem.at[1], recv_sem=yr_sem.at[u, half],
            device_id=(device(ROW if half else -ROW), tm), device_id_type=MESH,
        )

    def then_y(u, half):
        c, p = u // PIECES, lax.rem(u, PIECES)
        return pltpu.make_async_remote_copy(
            src_ref=relay.at[0, c, p], dst_ref=(up if half else down).at[c, p, pl.ds(0, 2)],
            send_sem=rs_sem.at[0], recv_sem=yr_sem.at[u, half],
            device_id=(device(1 - ROW if half else ROW - 1), tm), device_id_type=MESH,
        )

    down_here, up_here = jnp.logical_not(first), jnp.logical_not(last)
    inner = ((0, down_here), (1, up_here))
    edges = ((0, jnp.logical_and(first, low)), (1, jnp.logical_and(last, high)))
    turns_z = ((0, jnp.logical_and(last, low)), (1, jnp.logical_and(first, high)))
    turns_y = ((0, jnp.logical_and(first, high)), (1, jnp.logical_and(last, low)))

    def halo_start(u):
        for half, wanted in edges:

            @pl.when(wanted)
            def _():
                cross_z(u, half).start()
                cross_y(u, half).start()

        for half, wanted in inner:

            @pl.when(wanted)
            def _():
                straight(u, half).start()

    def pass_on(u):
        for half, wanted in turns_z:

            @pl.when(wanted)
            def _():
                cross_y(u, half).wait_recv()
                then_z(u, half).start()

        for half, wanted in turns_y:

            @pl.when(wanted)
            def _():
                cross_z(u, half).wait_recv()
                then_y(u, half).start()

    def halo_arrived(u):
        for half, wanted in ((0, has_after), (1, has_before)):

            @pl.when(wanted)
            def _():
                straight(u, half).wait_recv()

    def halo_sent():
        for half, wanted in ((0, has_before), (1, has_after)):
            whole = up if half else down

            @pl.when(wanted)
            def _():
                pltpu.make_async_remote_copy(
                    src_ref=whole, dst_ref=whole, send_sem=ys_sem.at[half],
                    recv_sem=yr_sem.at[0, half],
                    device_id=(device(1 if half else -1), tm), device_id_type=MESH,
                ).wait_send()

        for part, turns in ((1, turns_z), (0, turns_y)):
            for half, wanted in turns:
                whole = relay.at[part]

                @pl.when(wanted)
                def _():
                    pltpu.make_async_remote_copy(
                        src_ref=whole, dst_ref=whole, send_sem=rs_sem.at[part],
                        recv_sem=yr_sem.at[0, half],
                        device_id=(device(1 if half else -1), tm), device_id_type=MESH,
                    ).wait_send()

    def mate_send(c):
        return pltpu.make_async_remote_copy(
            src_ref=mine.at[c], dst_ref=mates.at[c],
            send_sem=ms_sem.at[c], recv_sem=mr_sem.at[c],
            device_id=(chan, mate), device_id_type=MESH,
        )

    def row_result(c, i, t):
        return pltpu.make_async_remote_copy(
            src_ref=lag.at[i, c], dst_ref=from_row.at[t, c],
            send_sem=os_sem.at[c, 0], recv_sem=or_sem.at[c, 0],
            device_id=(device(0, i), x), device_id_type=MESH,
        )

    def next_result(c, i, t):
        at = pl.ds(16, 16) if i < 2 else pl.ds(0, 32)
        return pltpu.make_async_remote_copy(
            src_ref=lag.at[i, c, at], dst_ref=from_next.at[t, c, at],
            send_sem=os_sem.at[c, 1], recv_sem=or_sem.at[c, 1],
            device_id=(device(-1, i), x), device_id_type=MESH,
        )

    def whiten(c, half):
        @pl.when(half == 0)
        def _():
            rec_copy(c).wait()

        data = rec[c, :, half].reshape(128, LEN)
        reals, imags, mags = [], [], []
        for p in range(PIECES):
            if isinstance(c, int) and c == 0 and half == 0:
                fwd_copy(p).wait()
            spectrum = jnp.dot(data, fwd[p], preferred_element_type=F32)
            real, imag = spectrum[:, :WIDE], spectrum[:, WIDE:]
            reals.append(real)
            imags.append(imag)
            mags.append(jnp.sqrt(real * real + imag * imag))
        water = sum(jnp.sum(mag, axis=1, keepdims=True) for mag in mags) * (1.0 / FREQ)
        floor = 0.1 * water + 1e-06
        for p in range(PIECES):
            inverse = 1.0 / (mags[p] + floor)
            for at, part in ((0, reals[p]), (WIDE, imags[p])):
                white = (part * inverse).astype(BF16).reshape(ROW, 32, WIDE)
                for there in range(ROW):
                    own[there, c, p, half, :, at : at + WIDE] = white[there]
        for p in range(PIECES):
            held[c, p, half, x] = own[x, c, p, half]

    sub = lax.broadcasted_iota(jnp.int32, (8, 128), 0)

    def correlate(c, p):
        for lane in range(0, WIDE, 128):

            def load(ref, *at):
                both = []
                for lanes in (lane, WIDE + lane):
                    part = ref[*at, :, lanes : lanes + 128].astype(F32)
                    both.append([part[8 * n : 8 * n + 8] for n in range(4)])
                return list(zip(*both))

            here = [[load(held, c, p, half, i) for i in range(ROW)] for half in range(2)]
            after = [load(down, c, p, i) for i in range(ROW)]
            before = [load(up, c, p, i) for i in range(ROW)]
            for i in range(ROW):
                for offset in range(1, REACH + 1):
                    q = i + offset
                    if q < ROW:
                        lefts = here[0][i] + here[1][i]
                        rights = here[0][q] + here[1][q]
                    else:
                        lefts = here[0][i] + before[i]
                        rights = after[q - ROW] + here[1][q - ROW]
                    pairs = list(zip(lefts, rights))
                    reals = [ar * pr + ai * pi for (ar, ai), (pr, pi) in pairs]
                    imags = [ai * pr - ar * pi for (ar, ai), (pr, pi) in pairs]
                    at = (i * REACH + offset - 1) * 8
                    cross[at : at + 8, lane : lane + 128] = gather_rows(reals, sub)
                    cross[at : at + 8, WIDE + lane : WIDE + lane + 128] = gather_rows(imags, sub)

        whole = cross[...]
        high = whole.astype(BF16)
        low = (whole - high.astype(F32)).astype(BF16)
        first = jnp.dot(high, inv[p], preferred_element_type=F32)
        second = jnp.dot(low, inv[p, :, :LAGS], preferred_element_type=F32)
        term = first[:, :LAGS] + (first[:, LAGS:] + second)

        @pl.when(p == 0)
        def _():
            total[...] = term

        @pl.when(p > 0)
        def _():
            total[...] += term

    def keep_results(c):
        mine[c] = total[...] * scale

        @pl.when(jnp.logical_not(sums))
        def _():
            mate_send(c).start()

    def send_results(c):
        @pl.when(sums)
        def _():
            mate_send(c).wait_recv()
            for i in range(ROW):
                at = pl.ds(32 * i, 32)
                lag[i, c] = (mine[c, at] + mates[c, at]).astype(lag.dtype)

                @pl.when(jnp.logical_or(x != tm, x != i))
                def _():
                    row_result(c, i, pair).start()

                @pl.when(jnp.logical_and(x == tm, x == i))
                def _():
                    from_row[pair, c] = lag[i, c]

                @pl.when(has_before)
                def _():
                    next_result(c, i, pair).start()

    def results_wait(c, kind, part):
        return pltpu.make_async_remote_copy(
            src_ref=part, dst_ref=part, send_sem=os_sem.at[c, kind], recv_sem=or_sem.at[c, kind],
            device_id=(device(-1 if kind else 0, x), x), device_id_type=MESH,
        )

    def results_sent(c):
        @pl.when(sums)
        def _():
            @pl.when(x != tm)
            def _():
                results_wait(c, 0, lag.at[:, c]).wait_send()

            @pl.when(x == tm)
            def _():
                results_wait(c, 0, lag.at[pl.ds(0, ROW - 1), c]).wait_send()

            @pl.when(has_before)
            def _():
                results_wait(c, 1, lag.at[pl.ds(0, ROW - 1), c]).wait_send()

        @pl.when(jnp.logical_not(sums))
        def _():
            mate_send(c).wait_send()

    def results_arrived(c):
        @pl.when(x != tm)
        def _():
            results_wait(c, 0, from_row.at[:, c]).wait_recv()

        @pl.when(x == tm)
        def _():
            results_wait(c, 0, from_row.at[pl.ds(0, 1), c]).wait_recv()

        @pl.when(jnp.logical_and(has_after, x < 2))
        def _():
            results_wait(c, 1, from_next.at[:, c, pl.ds(16, 16)]).wait_recv()

        @pl.when(jnp.logical_and(has_after, x >= 2))
        def _():
            results_wait(c, 1, from_next.at[:, c]).wait_recv()

    @pl.when(jnp.logical_not(has_before))
    def _():
        @pl.loop(0, CHUNKS)
        def _(c):
            up[c] = jnp.zeros(up.shape[1:], up.dtype)

    @pl.when(jnp.logical_not(has_after))
    def _():
        @pl.loop(0, CHUNKS)
        def _(c):
            down[c] = jnp.zeros(down.shape[1:], down.dtype)

    def x_start(u, half=None):
        for d in (2, 1, 3):
            x_send(u, d, half).start()

    early = PIECES // 2 + 1
    whiten(0, 0)
    inv_copy.start()
    for c in range(1, CHUNKS):
        rec_copy(c).start()
    pl.semaphore_wait(barrier, peers)
    for u in range(early):
        x_start(u, 0)
    whiten(0, 1)
    for u in range(early):
        x_start(u, 1)
    for u in range(early, PIECES):
        x_start(u)
    inv_copy.wait()

    @pl.loop(0, UNITS + USE)
    def _(u):
        @pl.when(u < UNITS)
        def _():
            x_arrived(u)
            halo_start(u)

        @pl.when(jnp.logical_and(u >= PASS, u < UNITS + PASS))
        def _():
            pass_on(u - PASS)

        ahead, part = u // 2 + 1, lax.rem(u, 2)

        @pl.when(ahead < CHUNKS)
        def _():
            whiten(ahead, part)

        @pl.when(jnp.logical_and(ahead < CHUNKS, part == 1))
        def _():
            for p in range(PIECES):
                x_start(ahead * PIECES + p)

        @pl.when(u >= USE)
        def _():
            k = u - USE
            c, p = k // PIECES, lax.rem(k, PIECES)
            halo_arrived(k)
            correlate(c, p)

            @pl.when(p == PIECES - 1)
            def _():
                keep_results(c)

            @pl.when(jnp.logical_and(p == 0, c > 0))
            def _():
                send_results(c - 1)

    send_results(CHUNKS - 1)
    x_sent()
    halo_sent()
    for c in range(CHUNKS):
        results_arrived(c)
        for offset in range(1, REACH + 1):
            within = jnp.logical_or(sub < 4, x + offset < ROW)
            at = pl.ds((offset - 1) * 8, 8)
            terms = [
                jnp.where(within, from_row[t, c, at].astype(F32), from_next[t, c, at].astype(F32))
                for t in range(TM // 2)
            ]
            out_ref[offset - 1, 8 * c : 8 * c + 8] = terms[0] + terms[1]
    for c in range(CHUNKS):
        results_sent(c)


def body(records, partners):
    channels, windows, length = records.shape
    total_windows = windows * lax.axis_size("tm")
    scale = 1.0 / math.sqrt(total_windows * FREQ)
    dma = pltpu.SemaphoreType.DMA
    lagged = pl.pallas_call(
        functools.partial(kernel, scale),
        out_shape=jax.ShapeDtypeStruct((REACH, channels // TM, LAGS), F32),
        in_specs=[pl.BlockSpec(memory_space=pl.ANY)] * 3,
        out_specs=pl.BlockSpec(memory_space=pltpu.VMEM),
        scratch_shapes=[
            pltpu.VMEM((CHUNKS, ROW, 2, 4, windows, length), BF16),
            pltpu.VMEM((PIECES, LEN, 2 * WIDE), BF16),
            pltpu.VMEM((PIECES, 2 * WIDE, 2 * LAGS), BF16),
            pltpu.VMEM((ROW, CHUNKS, PIECES, 2, 32, 2 * WIDE), BF16),
            pltpu.VMEM((CHUNKS, PIECES, 2, ROW, 32, 2 * WIDE), BF16),
            pltpu.VMEM((CHUNKS, PIECES, ROW, 32, 2 * WIDE), BF16),
            pltpu.VMEM((CHUNKS, PIECES, ROW, 32, 2 * WIDE), BF16),
            pltpu.VMEM((2, CHUNKS, PIECES, 2, 32, 2 * WIDE), BF16),
            pltpu.VMEM((128, 2 * WIDE), F32),
            pltpu.VMEM((128, LAGS), F32),
            pltpu.VMEM((CHUNKS, 128, LAGS), F32),
            pltpu.VMEM((CHUNKS, 128, LAGS), F32),
            pltpu.VMEM((ROW, CHUNKS, 32, LAGS), RESULT),
            pltpu.VMEM((TM // 2, CHUNKS, 32, LAGS), RESULT),
            pltpu.VMEM((TM // 2, CHUNKS, 32, LAGS), RESULT),
            dma((CHUNKS,)), dma((PIECES,)), dma,
            dma, dma((UNITS,)),
            dma((2,)), dma((UNITS, 2)),
            dma((2,)), dma((UNITS, 2)),
            dma((CHUNKS,)), dma((CHUNKS,)),
            dma((CHUNKS, 2)), dma((CHUNKS, 2)),
        ],
        compiler_params=pltpu.CompilerParams(
            collective_id=0, has_side_effects=True, vmem_limit_bytes=56 << 20
        ),
        cost_estimate=pl.CostEstimate(
            flops=7 * 10**9, bytes_accessed=12 * 10**6, transcendentals=10**6
        ),
    )(
        records.reshape(ROW, CHUNKS, 2, channels // (ROW * CHUNKS * 2), windows, length),
        jnp.asarray(forward_matrix()),
        jnp.asarray(inverse_matrix()),
    )
    offsets = partners[0] - lax.axis_index("chan")
    chosen = 0.0
    for k in range(REACH):
        chosen = chosen + jnp.where((offsets == k + 1)[:, None, None], lagged[k][None], 0.0)
    return chosen[None]


def solution(mesh):
    return jax.shard_map(
        body,
        mesh=mesh,
        in_specs=(P("chan", "tm", None), P("chan", None)),
        out_specs=P("chan", None, "tm", None),
        check_vma=False,
    )
```

```python
import functools
import math

import jax
import jax.numpy as jnp
import numpy as np
from jax import lax
from jax.experimental import pallas as pl
from jax.experimental.pallas import tpu as pltpu
from jax.sharding import PartitionSpec as P

FREQ = 768
LAGS = 128
REACH = 4
LEN = 1920
ROW = 4
TM = 4
CHUNKS = 4
PIECES = 3
UNITS = CHUNKS * PIECES
PASS, USE = 2, 5
WIDE = FREQ // PIECES
MESH = pl.DeviceIdType.MESH
F32 = jnp.float32
BF16 = jnp.bfloat16
RESULT = jnp.bfloat16


def forward_matrix():
    times = np.arange(LEN, dtype=np.int64)[:, None]
    bins = np.arange(1, FREQ + 1, dtype=np.int64)[None, :]
    angle = 2.0 * math.pi / LEN * (times * bins % LEN)
    real, imag = np.cos(angle), -np.sin(angle)
    pieces = [
        np.concatenate([real[:, p * WIDE : (p + 1) * WIDE], imag[:, p * WIDE : (p + 1) * WIDE]], 1)
        for p in range(PIECES)
    ]
    return np.stack(pieces).astype(np.float32).astype(BF16)


def inverse_matrix():
    bins = np.arange(1, FREQ + 1, dtype=np.int64)[:, None]
    shifts = np.arange(LAGS, dtype=np.int64)[None, :] - LAGS // 2
    angle = 2.0 * math.pi / LEN * (bins * shifts % LEN)
    whole = np.concatenate([np.cos(angle), -np.sin(angle)], 0).astype(np.float32)
    high = whole.astype(BF16)
    low = (whole - high.astype(np.float32)).astype(BF16)
    both = np.concatenate([high, low], 1).reshape(2, PIECES, WIDE, 2 * LAGS)
    return both.transpose(1, 0, 2, 3).reshape(PIECES, 2 * WIDE, 2 * LAGS)


def gather_rows(tiles, sub):
    for shift in (1, 2, 4):
        mask = (sub & shift) == 0
        tiles = [
            jnp.where(mask, a, b) + pltpu.roll(jnp.where(mask, b, a), 8 - shift, 0)
            for a, b in zip(tiles[::2], tiles[1::2])
        ]
    return tiles[0]


def kernel(
    scale, rec_hbm, fwd_hbm, inv_hbm, out_ref,
    rec, fwd, inv, own, held, down, up, relay, cross, total, mine, mates, lag, from_row, from_next,
    rec_sem, fwd_sem, inv_sem, xs_sem, xr_sem, ys_sem, yr_sem, rs_sem, rr_sem, ms_sem, mr_sem, os_sem, or_sem,
):
    chan, tm = lax.axis_index("chan"), lax.axis_index("tm")
    rows = lax.axis_size("chan") // ROW
    planes = rows // ROW
    x, row = lax.rem(chan, ROW), chan // ROW
    y, plane = lax.rem(row, ROW), row // ROW
    has_before, has_after = row > 0, row < rows - 1
    core, pair = lax.rem(tm, 2), tm // 2
    mate = tm + 1 - 2 * core
    sums = lax.rem(x + tm, 2) == 0
    first, last = y == 0, y == ROW - 1
    low, high = plane > 0, plane < planes - 1

    def device(by, at=x):
        return lax.rem(row + rows + by, rows) * ROW + at

    def fwd_copy(p):
        return pltpu.make_async_copy(fwd_hbm.at[p], fwd.at[p], fwd_sem.at[p])

    def rec_copy(c):
        return pltpu.make_async_copy(rec_hbm.at[:, c], rec.at[c], rec_sem.at[c])

    rec_copy(0).start()
    for p in range(PIECES):
        fwd_copy(p).start()
    inv_copy = pltpu.make_async_copy(inv_hbm, inv, inv_sem)

    from_next[...] = jnp.zeros(from_next.shape, from_next.dtype)
    barrier = pltpu.get_barrier_semaphore()

    def greet(*there):
        pl.semaphore_signal(barrier, inc=1, device_id=there, device_id_type=MESH)

    for d in range(1, ROW):
        greet(device(0, lax.rem(x + d, ROW)), tm)
    for t in range(TM // 2):

        @pl.when(jnp.logical_or(x != tm, pair != t))
        def _():
            greet(device(0, tm), 2 * t + core)

    @pl.when(sums)
    def _():
        greet(chan, mate)

    @pl.when(jnp.logical_not(first))
    def _():
        greet(device(-1), tm)

    @pl.when(jnp.logical_not(last))
    def _():
        greet(device(1), tm)

    @pl.when(has_after)
    def _():
        for t in range(TM // 2):
            greet(device(1, tm), 2 * t + core)

    for at_edge, near in ((first, ROW - 1), (last, 1 - ROW)):
        for there, far in ((low, -ROW), (high, ROW)):

            @pl.when(jnp.logical_and(at_edge, there))
            def _():
                greet(device(near), tm)
                greet(device(far), tm)

    itself = 1 - ((x - tm) * (x - tm) + 15) // 16
    before = (row + rows - 1) // rows
    edge = ((2 * y - 3) * (2 * y - 3)) // 9
    around = (plane + planes - 1) // planes + 1 - (plane + 1) // planes
    other = lax.rem(x + tm, 2)
    results = other + (1 - other) * (ROW - itself + ROW * before)
    peers = ROW - 1 + results + 2 - edge + 2 * edge * around

    def x_send(u, d, half=None):
        c, p = u // PIECES, lax.rem(u, PIECES)
        there = lax.rem(x + d, ROW)
        at = (c, p) if half is None else (c, p, half)
        to = held.at[c, p, :, x] if half is None else held.at[c, p, half, x]
        return pltpu.make_async_remote_copy(
            src_ref=own.at[there, *at], dst_ref=to, send_sem=xs_sem, recv_sem=xr_sem.at[u],
            device_id=(device(0, there), tm), device_id_type=MESH,
        )

    def x_arrived(u):
        part = held.at[u // PIECES, lax.rem(u, PIECES), :, pl.ds(0, ROW - 1)]
        pltpu.make_async_remote_copy(
            src_ref=part, dst_ref=part, send_sem=xs_sem, recv_sem=xr_sem.at[u],
            device_id=(device(0, lax.rem(x + 1, ROW)), tm), device_id_type=MESH,
        ).wait_recv()

    def x_sent():
        part = own.at[pl.ds(0, ROW - 1)]
        pltpu.make_async_remote_copy(
            src_ref=part, dst_ref=part, send_sem=xs_sem, recv_sem=xr_sem.at[0],
            device_id=(device(0, lax.rem(x + 1, ROW)), tm), device_id_type=MESH,
        ).wait_send()

    def straight(u, half):
        c, p = u // PIECES, lax.rem(u, PIECES)
        return pltpu.make_async_remote_copy(
            src_ref=held.at[c, p, half], dst_ref=(up if half else down).at[c, p],
            send_sem=ys_sem.at[half], recv_sem=yr_sem.at[u, half],
            device_id=(device(1 if half else -1), tm), device_id_type=MESH,
        )

    def cross_y(u, half):
        c, p = u // PIECES, lax.rem(u, PIECES)
        return pltpu.make_async_remote_copy(
            src_ref=held.at[c, p, half, pl.ds(2, 2)], dst_ref=relay.at[1, c, p],
            send_sem=ys_sem.at[half], recv_sem=rr_sem.at[u, 1],
            device_id=(device(1 - ROW if half else ROW - 1), tm), device_id_type=MESH,
        )

    def cross_z(u, half):
        c, p = u // PIECES, lax.rem(u, PIECES)
        return pltpu.make_async_remote_copy(
            src_ref=held.at[c, p, half, pl.ds(0, 2)], dst_ref=relay.at[0, c, p],
            send_sem=ys_sem.at[half], recv_sem=rr_sem.at[u, 0],
            device_id=(device(ROW if half else -ROW), tm), device_id_type=MESH,
        )

    def then_z(u, half):
        c, p = u // PIECES, lax.rem(u, PIECES)
        return pltpu.make_async_remote_copy(
            src_ref=relay.at[1, c, p], dst_ref=(up if half else down).at[c, p, pl.ds(2, 2)],
            send_sem=rs_sem.at[1], recv_sem=yr_sem.at[u, half],
            device_id=(device(ROW if half else -ROW), tm), device_id_type=MESH,
        )

    def then_y(u, half):
        c, p = u // PIECES, lax.rem(u, PIECES)
        return pltpu.make_async_remote_copy(
            src_ref=relay.at[0, c, p], dst_ref=(up if half else down).at[c, p, pl.ds(0, 2)],
            send_sem=rs_sem.at[0], recv_sem=yr_sem.at[u, half],
            device_id=(device(1 - ROW if half else ROW - 1), tm), device_id_type=MESH,
        )

    down_here, up_here = jnp.logical_not(first), jnp.logical_not(last)
    inner = ((0, down_here), (1, up_here))
    edges = ((0, jnp.logical_and(first, low)), (1, jnp.logical_and(last, high)))
    turns_z = ((0, jnp.logical_and(last, low)), (1, jnp.logical_and(first, high)))
    turns_y = ((0, jnp.logical_and(first, high)), (1, jnp.logical_and(last, low)))

    def halo_start(u):
        for half, wanted in edges:

            @pl.when(wanted)
            def _():
                cross_z(u, half).start()
                cross_y(u, half).start()

        for half, wanted in inner:

            @pl.when(wanted)
            def _():
                straight(u, half).start()

    def pass_on(u):
        for half, wanted in turns_z:

            @pl.when(wanted)
            def _():
                cross_y(u, half).wait_recv()
                then_z(u, half).start()

        for half, wanted in turns_y:

            @pl.when(wanted)
            def _():
                cross_z(u, half).wait_recv()
                then_y(u, half).start()

    def halo_arrived(u):
        for half, wanted in ((0, has_after), (1, has_before)):

            @pl.when(wanted)
            def _():
                straight(u, half).wait_recv()

    def halo_sent():
        for half, wanted in ((0, has_before), (1, has_after)):
            whole = up if half else down

            @pl.when(wanted)
            def _():
                pltpu.make_async_remote_copy(
                    src_ref=whole, dst_ref=whole, send_sem=ys_sem.at[half],
                    recv_sem=yr_sem.at[0, half],
                    device_id=(device(1 if half else -1), tm), device_id_type=MESH,
                ).wait_send()

        for part, turns in ((1, turns_z), (0, turns_y)):
            for half, wanted in turns:
                whole = relay.at[part]

                @pl.when(wanted)
                def _():
                    pltpu.make_async_remote_copy(
                        src_ref=whole, dst_ref=whole, send_sem=rs_sem.at[part],
                        recv_sem=yr_sem.at[0, half],
                        device_id=(device(1 if half else -1), tm), device_id_type=MESH,
                    ).wait_send()

    def mate_send(c):
        return pltpu.make_async_remote_copy(
            src_ref=mine.at[c], dst_ref=mates.at[c],
            send_sem=ms_sem.at[c], recv_sem=mr_sem.at[c],
            device_id=(chan, mate), device_id_type=MESH,
        )

    def row_result(c, i, t):
        return pltpu.make_async_remote_copy(
            src_ref=lag.at[i, c], dst_ref=from_row.at[t, c],
            send_sem=os_sem.at[c, 0], recv_sem=or_sem.at[c, 0],
            device_id=(device(0, i), x), device_id_type=MESH,
        )

    def next_result(c, i, t):
        at = pl.ds(16, 16) if i < 2 else pl.ds(0, 32)
        return pltpu.make_async_remote_copy(
            src_ref=lag.at[i, c, at], dst_ref=from_next.at[t, c, at],
            send_sem=os_sem.at[c, 1], recv_sem=or_sem.at[c, 1],
            device_id=(device(-1, i), x), device_id_type=MESH,
        )

    def whiten(c, half):
        @pl.when(half == 0)
        def _():
            rec_copy(c).wait()

        data = rec[c, :, half].reshape(128, LEN)
        reals, imags, mags = [], [], []
        for p in range(PIECES):
            if isinstance(c, int) and c == 0 and half == 0:
                fwd_copy(p).wait()
            spectrum = jnp.dot(data, fwd[p], preferred_element_type=F32)
            real, imag = spectrum[:, :WIDE], spectrum[:, WIDE:]
            reals.append(real)
            imags.append(imag)
            mags.append(jnp.sqrt(real * real + imag * imag))
        water = sum(jnp.sum(mag, axis=1, keepdims=True) for mag in mags) * (1.0 / FREQ)
        floor = 0.1 * water + 1e-06
        for p in range(PIECES):
            inverse = 1.0 / (mags[p] + floor)
            for at, part in ((0, reals[p]), (WIDE, imags[p])):
                white = (part * inverse).astype(BF16).reshape(ROW, 32, WIDE)
                for there in range(ROW):
                    own[there, c, p, half, :, at : at + WIDE] = white[there]
        for p in range(PIECES):
            held[c, p, half, x] = own[x, c, p, half]

    sub = lax.broadcasted_iota(jnp.int32, (8, 128), 0)

    def correlate(c, p):
        for lane in range(0, WIDE, 128):

            def load(ref, *at):
                both = []
                for lanes in (lane, WIDE + lane):
                    part = ref[*at, :, lanes : lanes + 128].astype(F32)
                    both.append([part[8 * n : 8 * n + 8] for n in range(4)])
                return list(zip(*both))

            here = [[load(held, c, p, half, i) for i in range(ROW)] for half in range(2)]
            after = [load(down, c, p, i) for i in range(ROW)]
            before = [load(up, c, p, i) for i in range(ROW)]
            for i in range(ROW):
                for offset in range(1, REACH + 1):
                    q = i + offset
                    if q < ROW:
                        lefts = here[0][i] + here[1][i]
                        rights = here[0][q] + here[1][q]
                    else:
                        lefts = here[0][i] + before[i]
                        rights = after[q - ROW] + here[1][q - ROW]
                    pairs = list(zip(lefts, rights))
                    reals = [ar * pr + ai * pi for (ar, ai), (pr, pi) in pairs]
                    imags = [ai * pr - ar * pi for (ar, ai), (pr, pi) in pairs]
                    at = (i * REACH + offset - 1) * 8
                    cross[at : at + 8, lane : lane + 128] = gather_rows(reals, sub)
                    cross[at : at + 8, WIDE + lane : WIDE + lane + 128] = gather_rows(imags, sub)

        whole = cross[...]
        high = whole.astype(BF16)
        low = (whole - high.astype(F32)).astype(BF16)
        first = jnp.dot(high, inv[p], preferred_element_type=F32)
        second = jnp.dot(low, inv[p, :, :LAGS], preferred_element_type=F32)
        term = first[:, :LAGS] + (first[:, LAGS:] + second)

        @pl.when(p == 0)
        def _():
            total[...] = term

        @pl.when(p > 0)
        def _():
            total[...] += term

    def keep_results(c):
        mine[c] = total[...] * scale

        @pl.when(jnp.logical_not(sums))
        def _():
            mate_send(c).start()

    def send_results(c):
        @pl.when(sums)
        def _():
            mate_send(c).wait_recv()
            for i in range(ROW):
                at = pl.ds(32 * i, 32)
                lag[i, c] = (mine[c, at] + mates[c, at]).astype(lag.dtype)

                @pl.when(jnp.logical_or(x != tm, x != i))
                def _():
                    row_result(c, i, pair).start()

                @pl.when(jnp.logical_and(x == tm, x == i))
                def _():
                    from_row[pair, c] = lag[i, c]

                @pl.when(has_before)
                def _():
                    next_result(c, i, pair).start()

    def results_wait(c, kind, part):
        return pltpu.make_async_remote_copy(
            src_ref=part, dst_ref=part, send_sem=os_sem.at[c, kind], recv_sem=or_sem.at[c, kind],
            device_id=(device(-1 if kind else 0, x), x), device_id_type=MESH,
        )

    def results_sent(c):
        @pl.when(sums)
        def _():
            @pl.when(x != tm)
            def _():
                results_wait(c, 0, lag.at[:, c]).wait_send()

            @pl.when(x == tm)
            def _():
                results_wait(c, 0, lag.at[pl.ds(0, ROW - 1), c]).wait_send()

            @pl.when(has_before)
            def _():
                results_wait(c, 1, lag.at[pl.ds(0, ROW - 1), c]).wait_send()

        @pl.when(jnp.logical_not(sums))
        def _():
            mate_send(c).wait_send()

    def results_arrived(c):
        @pl.when(x != tm)
        def _():
            results_wait(c, 0, from_row.at[:, c]).wait_recv()

        @pl.when(x == tm)
        def _():
            results_wait(c, 0, from_row.at[pl.ds(0, 1), c]).wait_recv()

        @pl.when(jnp.logical_and(has_after, x < 2))
        def _():
            results_wait(c, 1, from_next.at[:, c, pl.ds(16, 16)]).wait_recv()

        @pl.when(jnp.logical_and(has_after, x >= 2))
        def _():
            results_wait(c, 1, from_next.at[:, c]).wait_recv()

    @pl.when(jnp.logical_not(has_before))
    def _():
        @pl.loop(0, CHUNKS)
        def _(c):
            up[c] = jnp.zeros(up.shape[1:], up.dtype)

    @pl.when(jnp.logical_not(has_after))
    def _():
        @pl.loop(0, CHUNKS)
        def _(c):
            down[c] = jnp.zeros(down.shape[1:], down.dtype)

    def x_start(u, half=None):
        for d in (2, 1, 3):
            x_send(u, d, half).start()

    early = PIECES // 2 + 1
    whiten(0, 0)
    inv_copy.start()
    for c in range(1, CHUNKS):
        rec_copy(c).start()
    pl.semaphore_wait(barrier, peers)
    for u in range(early):
        x_start(u, 0)
    whiten(0, 1)
    for u in range(early):
        x_start(u, 1)
    for u in range(early, PIECES):
        x_start(u)
    inv_copy.wait()

    @pl.loop(0, UNITS + USE)
    def _(u):
        @pl.when(u < UNITS)
        def _():
            x_arrived(u)
            halo_start(u)

        @pl.when(jnp.logical_and(u >= PASS, u < UNITS + PASS))
        def _():
            pass_on(u - PASS)

        ahead, part = u // 2 + 1, lax.rem(u, 2)

        @pl.when(ahead < CHUNKS)
        def _():
            whiten(ahead, part)

        @pl.when(jnp.logical_and(ahead < CHUNKS, part == 1))
        def _():
            for p in range(PIECES):
                x_start(ahead * PIECES + p)

        @pl.when(u >= USE)
        def _():
            k = u - USE
            c, p = k // PIECES, lax.rem(k, PIECES)
            halo_arrived(k)
            correlate(c, p)

            @pl.when(p == PIECES - 1)
            def _():
                keep_results(c)

            @pl.when(jnp.logical_and(p == 0, c > 0))
            def _():
                send_results(c - 1)

    send_results(CHUNKS - 1)
    x_sent()
    halo_sent()
    for c in range(CHUNKS):
        results_arrived(c)
        inside = from_row[0, c].astype(F32) + from_row[1, c].astype(F32)
        beyond = from_next[0, c].astype(F32) + from_next[1, c].astype(F32)
        for offset in range(1, REACH + 1):
            within = jnp.logical_or(sub < 4, x + offset < ROW)
            at = (offset - 1) * 8
            tile = jnp.where(within, inside[at : at + 8], beyond[at : at + 8])
            out_ref[offset - 1, 8 * c : 8 * c + 8] = tile
    for c in range(CHUNKS):
        results_sent(c)


def body(records, partners):
    channels, windows, length = records.shape
    total_windows = windows * lax.axis_size("tm")
    scale = 1.0 / math.sqrt(total_windows * FREQ)
    dma = pltpu.SemaphoreType.DMA
    lagged = pl.pallas_call(
        functools.partial(kernel, scale),
        out_shape=jax.ShapeDtypeStruct((REACH, channels // TM, LAGS), F32),
        in_specs=[pl.BlockSpec(memory_space=pl.ANY)] * 3,
        out_specs=pl.BlockSpec(memory_space=pltpu.VMEM),
        scratch_shapes=[
            pltpu.VMEM((CHUNKS, ROW, 2, 4, windows, length), BF16),
            pltpu.VMEM((PIECES, LEN, 2 * WIDE), BF16),
            pltpu.VMEM((PIECES, 2 * WIDE, 2 * LAGS), BF16),
            pltpu.VMEM((ROW, CHUNKS, PIECES, 2, 32, 2 * WIDE), BF16),
            pltpu.VMEM((CHUNKS, PIECES, 2, ROW, 32, 2 * WIDE), BF16),
            pltpu.VMEM((CHUNKS, PIECES, ROW, 32, 2 * WIDE), BF16),
            pltpu.VMEM((CHUNKS, PIECES, ROW, 32, 2 * WIDE), BF16),
            pltpu.VMEM((2, CHUNKS, PIECES, 2, 32, 2 * WIDE), BF16),
            pltpu.VMEM((128, 2 * WIDE), F32),
            pltpu.VMEM((128, LAGS), F32),
            pltpu.VMEM((CHUNKS, 128, LAGS), F32),
            pltpu.VMEM((CHUNKS, 128, LAGS), F32),
            pltpu.VMEM((ROW, CHUNKS, 32, LAGS), RESULT),
            pltpu.VMEM((TM // 2, CHUNKS, 32, LAGS), RESULT),
            pltpu.VMEM((TM // 2, CHUNKS, 32, LAGS), RESULT),
            dma((CHUNKS,)), dma((PIECES,)), dma,
            dma, dma((UNITS,)),
            dma((2,)), dma((UNITS, 2)),
            dma((2,)), dma((UNITS, 2)),
            dma((CHUNKS,)), dma((CHUNKS,)),
            dma((CHUNKS, 2)), dma((CHUNKS, 2)),
        ],
        compiler_params=pltpu.CompilerParams(
            collective_id=0, has_side_effects=True, vmem_limit_bytes=56 << 20
        ),
        cost_estimate=pl.CostEstimate(
            flops=7 * 10**9, bytes_accessed=12 * 10**6, transcendentals=10**6
        ),
    )(
        records.reshape(ROW, CHUNKS, 2, channels // (ROW * CHUNKS * 2), windows, length),
        jnp.asarray(forward_matrix()),
        jnp.asarray(inverse_matrix()),
    )
    offsets = partners[0] - lax.axis_index("chan")
    chosen = 0.0
    for k in range(REACH):
        chosen = chosen + jnp.where((offsets == k + 1)[:, None, None], lagged[k][None], 0.0)
    return chosen[None]


def solution(mesh):
    return jax.shard_map(
        body,
        mesh=mesh,
        in_specs=(P("chan", "tm", None), P("chan", None)),
        out_specs=P("chan", None, "tm", None),
        check_vma=False,
    )
```

```python
import functools
import math

import jax
import jax.numpy as jnp
import numpy as np
from jax import lax
from jax.experimental import pallas as pl
from jax.experimental.pallas import tpu as pltpu
from jax.sharding import PartitionSpec as P

FREQ = 768
LAGS = 128
REACH = 4
LEN = 1920
HALF, DEEP = LEN // 2, 1024
ROW = 4
TM = 4
CHUNKS = 4
PIECES = 3
UNITS = CHUNKS * PIECES
PASS, USE = 2, 5
WIDE = FREQ // PIECES
MESH = pl.DeviceIdType.MESH
F32 = jnp.float32
BF16 = jnp.bfloat16
RESULT = jnp.bfloat16


def bin_order():
    return np.concatenate([np.arange(2, FREQ + 1, 2), np.arange(1, FREQ + 1, 2)]).astype(np.int64)


def forward_matrix():
    times = np.arange(HALF, dtype=np.int64)[:, None]
    bins = bin_order()[None, :]
    angle = 2.0 * math.pi / LEN * (times * bins % LEN)
    real, imag = np.cos(angle), -np.sin(angle)
    pieces = [
        np.concatenate([real[:, p * WIDE : (p + 1) * WIDE], imag[:, p * WIDE : (p + 1) * WIDE]], 1)
        for p in range(PIECES)
    ]
    table = np.zeros((PIECES, DEEP, 2 * WIDE), np.float32)
    table[:, :HALF] = np.stack(pieces)
    return table.astype(BF16)


def inverse_matrix():
    bins = bin_order()[:, None]
    shifts = np.arange(LAGS, dtype=np.int64)[None, :] - LAGS // 2
    angle = 2.0 * math.pi / LEN * (bins * shifts % LEN)
    whole = np.concatenate([np.cos(angle), -np.sin(angle)], 0).astype(np.float32)
    high = whole.astype(BF16)
    low = (whole - high.astype(np.float32)).astype(BF16)
    both = np.concatenate([high, low], 1).reshape(2, PIECES, WIDE, 2 * LAGS)
    return both.transpose(1, 0, 2, 3).reshape(PIECES, 2 * WIDE, 2 * LAGS)


def gather_rows(tiles, sub):
    for shift in (1, 2, 4):
        mask = (sub & shift) == 0
        tiles = [
            jnp.where(mask, a, b) + pltpu.roll(jnp.where(mask, b, a), 8 - shift, 0)
            for a, b in zip(tiles[::2], tiles[1::2])
        ]
    return tiles[0]


def kernel(
    scale, rec_hbm, fwd_hbm, inv_hbm, out_ref,
    rec, fwd, inv, own, held, down, up, relay, cross, total, mine, mates, lag, from_row, from_next,
    rec_sem, fwd_sem, inv_sem, xs_sem, xr_sem, ys_sem, yr_sem, rs_sem, rr_sem, ms_sem, mr_sem, os_sem, or_sem,
):
    chan, tm = lax.axis_index("chan"), lax.axis_index("tm")
    rows = lax.axis_size("chan") // ROW
    planes = rows // ROW
    x, row = lax.rem(chan, ROW), chan // ROW
    y, plane = lax.rem(row, ROW), row // ROW
    has_before, has_after = row > 0, row < rows - 1
    core, pair = lax.rem(tm, 2), tm // 2
    mate = tm + 1 - 2 * core
    sums = lax.rem(x + tm, 2) == 0
    first, last = y == 0, y == ROW - 1
    low, high = plane > 0, plane < planes - 1

    def device(by, at=x):
        return lax.rem(row + rows + by, rows) * ROW + at

    def fwd_copy(p):
        return pltpu.make_async_copy(fwd_hbm.at[p], fwd.at[p], fwd_sem.at[p])

    def rec_copy(c):
        return pltpu.make_async_copy(rec_hbm.at[:, c], rec.at[c], rec_sem.at[c])

    rec_copy(0).start()
    for p in range(PIECES):
        fwd_copy(p).start()
    inv_copy = pltpu.make_async_copy(inv_hbm, inv, inv_sem)

    from_next[...] = jnp.zeros(from_next.shape, from_next.dtype)
    barrier = pltpu.get_barrier_semaphore()

    def greet(*there):
        pl.semaphore_signal(barrier, inc=1, device_id=there, device_id_type=MESH)

    for d in range(1, ROW):
        greet(device(0, lax.rem(x + d, ROW)), tm)
    for t in range(TM // 2):

        @pl.when(jnp.logical_or(x != tm, pair != t))
        def _():
            greet(device(0, tm), 2 * t + core)

    @pl.when(sums)
    def _():
        greet(chan, mate)

    @pl.when(jnp.logical_not(first))
    def _():
        greet(device(-1), tm)

    @pl.when(jnp.logical_not(last))
    def _():
        greet(device(1), tm)

    @pl.when(has_after)
    def _():
        for t in range(TM // 2):
            greet(device(1, tm), 2 * t + core)

    for at_edge, near in ((first, ROW - 1), (last, 1 - ROW)):
        for there, far in ((low, -ROW), (high, ROW)):

            @pl.when(jnp.logical_and(at_edge, there))
            def _():
                greet(device(near), tm)
                greet(device(far), tm)

    itself = 1 - ((x - tm) * (x - tm) + 15) // 16
    before = (row + rows - 1) // rows
    edge = ((2 * y - 3) * (2 * y - 3)) // 9
    around = (plane + planes - 1) // planes + 1 - (plane + 1) // planes
    other = lax.rem(x + tm, 2)
    results = other + (1 - other) * (ROW - itself + ROW * before)
    peers = ROW - 1 + results + 2 - edge + 2 * edge * around

    def x_send(u, d, half=None):
        c, p = u // PIECES, lax.rem(u, PIECES)
        there = lax.rem(x + d, ROW)
        at = (c, p) if half is None else (c, p, half)
        to = held.at[c, p, :, x] if half is None else held.at[c, p, half, x]
        return pltpu.make_async_remote_copy(
            src_ref=own.at[there, *at], dst_ref=to, send_sem=xs_sem, recv_sem=xr_sem.at[u],
            device_id=(device(0, there), tm), device_id_type=MESH,
        )

    def x_arrived(u):
        part = held.at[u // PIECES, lax.rem(u, PIECES), :, pl.ds(0, ROW - 1)]
        pltpu.make_async_remote_copy(
            src_ref=part, dst_ref=part, send_sem=xs_sem, recv_sem=xr_sem.at[u],
            device_id=(device(0, lax.rem(x + 1, ROW)), tm), device_id_type=MESH,
        ).wait_recv()

    def x_sent():
        part = own.at[pl.ds(0, ROW - 1)]
        pltpu.make_async_remote_copy(
            src_ref=part, dst_ref=part, send_sem=xs_sem, recv_sem=xr_sem.at[0],
            device_id=(device(0, lax.rem(x + 1, ROW)), tm), device_id_type=MESH,
        ).wait_send()

    def straight(u, half):
        c, p = u // PIECES, lax.rem(u, PIECES)
        return pltpu.make_async_remote_copy(
            src_ref=held.at[c, p, half], dst_ref=(up if half else down).at[c, p],
            send_sem=ys_sem.at[half], recv_sem=yr_sem.at[u, half],
            device_id=(device(1 if half else -1), tm), device_id_type=MESH,
        )

    def cross_y(u, half):
        c, p = u // PIECES, lax.rem(u, PIECES)
        return pltpu.make_async_remote_copy(
            src_ref=held.at[c, p, half, pl.ds(2, 2)], dst_ref=relay.at[1, c, p],
            send_sem=ys_sem.at[half], recv_sem=rr_sem.at[u, 1],
            device_id=(device(1 - ROW if half else ROW - 1), tm), device_id_type=MESH,
        )

    def cross_z(u, half):
        c, p = u // PIECES, lax.rem(u, PIECES)
        return pltpu.make_async_remote_copy(
            src_ref=held.at[c, p, half, pl.ds(0, 2)], dst_ref=relay.at[0, c, p],
            send_sem=ys_sem.at[half], recv_sem=rr_sem.at[u, 0],
            device_id=(device(ROW if half else -ROW), tm), device_id_type=MESH,
        )

    def then_z(u, half):
        c, p = u // PIECES, lax.rem(u, PIECES)
        return pltpu.make_async_remote_copy(
            src_ref=relay.at[1, c, p], dst_ref=(up if half else down).at[c, p, pl.ds(2, 2)],
            send_sem=rs_sem.at[1], recv_sem=yr_sem.at[u, half],
            device_id=(device(ROW if half else -ROW), tm), device_id_type=MESH,
        )

    def then_y(u, half):
        c, p = u // PIECES, lax.rem(u, PIECES)
        return pltpu.make_async_remote_copy(
            src_ref=relay.at[0, c, p], dst_ref=(up if half else down).at[c, p, pl.ds(0, 2)],
            send_sem=rs_sem.at[0], recv_sem=yr_sem.at[u, half],
            device_id=(device(1 - ROW if half else ROW - 1), tm), device_id_type=MESH,
        )

    down_here, up_here = jnp.logical_not(first), jnp.logical_not(last)
    inner = ((0, down_here), (1, up_here))
    edges = ((0, jnp.logical_and(first, low)), (1, jnp.logical_and(last, high)))
    turns_z = ((0, jnp.logical_and(last, low)), (1, jnp.logical_and(first, high)))
    turns_y = ((0, jnp.logical_and(first, high)), (1, jnp.logical_and(last, low)))

    def halo_start(u):
        for half, wanted in edges:

            @pl.when(wanted)
            def _():
                cross_z(u, half).start()
                cross_y(u, half).start()

        for half, wanted in inner:

            @pl.when(wanted)
            def _():
                straight(u, half).start()

    def pass_on(u):
        for half, wanted in turns_z:

            @pl.when(wanted)
            def _():
                cross_y(u, half).wait_recv()
                then_z(u, half).start()

        for half, wanted in turns_y:

            @pl.when(wanted)
            def _():
                cross_z(u, half).wait_recv()
                then_y(u, half).start()

    def halo_arrived(u):
        for half, wanted in ((0, has_after), (1, has_before)):

            @pl.when(wanted)
            def _():
                straight(u, half).wait_recv()

    def halo_sent():
        for half, wanted in ((0, has_before), (1, has_after)):
            whole = up if half else down

            @pl.when(wanted)
            def _():
                pltpu.make_async_remote_copy(
                    src_ref=whole, dst_ref=whole, send_sem=ys_sem.at[half],
                    recv_sem=yr_sem.at[0, half],
                    device_id=(device(1 if half else -1), tm), device_id_type=MESH,
                ).wait_send()

        for part, turns in ((1, turns_z), (0, turns_y)):
            for half, wanted in turns:
                whole = relay.at[part]

                @pl.when(wanted)
                def _():
                    pltpu.make_async_remote_copy(
                        src_ref=whole, dst_ref=whole, send_sem=rs_sem.at[part],
                        recv_sem=yr_sem.at[0, half],
                        device_id=(device(1 if half else -1), tm), device_id_type=MESH,
                    ).wait_send()

    def mate_send(c):
        return pltpu.make_async_remote_copy(
            src_ref=mine.at[c], dst_ref=mates.at[c],
            send_sem=ms_sem.at[c], recv_sem=mr_sem.at[c],
            device_id=(chan, mate), device_id_type=MESH,
        )

    def row_result(c, i, t):
        return pltpu.make_async_remote_copy(
            src_ref=lag.at[i, c], dst_ref=from_row.at[t, c],
            send_sem=os_sem.at[c, 0], recv_sem=or_sem.at[c, 0],
            device_id=(device(0, i), x), device_id_type=MESH,
        )

    def next_result(c, i, t):
        at = pl.ds(16, 16) if i < 2 else pl.ds(0, 32)
        return pltpu.make_async_remote_copy(
            src_ref=lag.at[i, c, at], dst_ref=from_next.at[t, c, at],
            send_sem=os_sem.at[c, 1], recv_sem=or_sem.at[c, 1],
            device_id=(device(-1, i), x), device_id_type=MESH,
        )

    def whiten(c, half):
        @pl.when(half == 0)
        def _():
            rec_copy(c).wait()

        data = rec[c, :, half].reshape(128, LEN)
        second = pltpu.roll(data[:, LEN - DEEP :], HALF, 1)
        data = jnp.concatenate([data[:, :DEEP], second], axis=0)
        reals, imags, mags = [], [], []
        for p in range(PIECES):
            if isinstance(c, int) and c == 0 and half == 0:
                fwd_copy(p).wait()
            spectrum = jnp.dot(data, fwd[p], preferred_element_type=F32)
            columns = []
            for at in range(0, 2 * WIDE, 128):
                before, after = spectrum[:128, at : at + 128], spectrum[128:, at : at + 128]
                even = 2 * (p * WIDE + at % WIDE) < FREQ
                columns.append(before + after if even else before - after)
            real = jnp.concatenate(columns[: WIDE // 128], axis=1)
            imag = jnp.concatenate(columns[WIDE // 128 :], axis=1)
            reals.append(real)
            imags.append(imag)
            mags.append(jnp.sqrt(real * real + imag * imag))
        water = sum(jnp.sum(mag, axis=1, keepdims=True) for mag in mags) * (1.0 / FREQ)
        floor = 0.1 * water + 1e-06
        for p in range(PIECES):
            inverse = 1.0 / (mags[p] + floor)
            for at, part in ((0, reals[p]), (WIDE, imags[p])):
                white = (part * inverse).astype(BF16).reshape(ROW, 32, WIDE)
                for there in range(ROW):
                    own[there, c, p, half, :, at : at + WIDE] = white[there]
        for p in range(PIECES):
            held[c, p, half, x] = own[x, c, p, half]

    sub = lax.broadcasted_iota(jnp.int32, (8, 128), 0)

    def correlate(c, p):
        for lane in range(0, WIDE, 128):

            def load(ref, *at):
                both = []
                for lanes in (lane, WIDE + lane):
                    part = ref[*at, :, lanes : lanes + 128].astype(F32)
                    both.append([part[8 * n : 8 * n + 8] for n in range(4)])
                return list(zip(*both))

            here = [[load(held, c, p, half, i) for i in range(ROW)] for half in range(2)]
            after = [load(down, c, p, i) for i in range(ROW)]
            before = [load(up, c, p, i) for i in range(ROW)]
            for i in range(ROW):
                for offset in range(1, REACH + 1):
                    q = i + offset
                    if q < ROW:
                        lefts = here[0][i] + here[1][i]
                        rights = here[0][q] + here[1][q]
                    else:
                        lefts = here[0][i] + before[i]
                        rights = after[q - ROW] + here[1][q - ROW]
                    pairs = list(zip(lefts, rights))
                    reals = [ar * pr + ai * pi for (ar, ai), (pr, pi) in pairs]
                    imags = [ai * pr - ar * pi for (ar, ai), (pr, pi) in pairs]
                    at = (i * REACH + offset - 1) * 8
                    cross[at : at + 8, lane : lane + 128] = gather_rows(reals, sub)
                    cross[at : at + 8, WIDE + lane : WIDE + lane + 128] = gather_rows(imags, sub)

        whole = cross[...]
        high = whole.astype(BF16)
        low = (whole - high.astype(F32)).astype(BF16)
        first = jnp.dot(high, inv[p], preferred_element_type=F32)
        second = jnp.dot(low, inv[p, :, :LAGS], preferred_element_type=F32)
        term = first[:, :LAGS] + (first[:, LAGS:] + second)

        @pl.when(p == 0)
        def _():
            total[...] = term

        @pl.when(p > 0)
        def _():
            total[...] += term

    def keep_results(c):
        mine[c] = total[...] * scale

        @pl.when(jnp.logical_not(sums))
        def _():
            mate_send(c).start()

    def send_results(c):
        @pl.when(sums)
        def _():
            mate_send(c).wait_recv()
            for i in range(ROW):
                at = pl.ds(32 * i, 32)
                lag[i, c] = (mine[c, at] + mates[c, at]).astype(lag.dtype)

                @pl.when(jnp.logical_or(x != tm, x != i))
                def _():
                    row_result(c, i, pair).start()

                @pl.when(jnp.logical_and(x == tm, x == i))
                def _():
                    from_row[pair, c] = lag[i, c]

                @pl.when(has_before)
                def _():
                    next_result(c, i, pair).start()

    def results_wait(c, kind, part):
        return pltpu.make_async_remote_copy(
            src_ref=part, dst_ref=part, send_sem=os_sem.at[c, kind], recv_sem=or_sem.at[c, kind],
            device_id=(device(-1 if kind else 0, x), x), device_id_type=MESH,
        )

    def results_sent(c):
        @pl.when(sums)
        def _():
            @pl.when(x != tm)
            def _():
                results_wait(c, 0, lag.at[:, c]).wait_send()

            @pl.when(x == tm)
            def _():
                results_wait(c, 0, lag.at[pl.ds(0, ROW - 1), c]).wait_send()

            @pl.when(has_before)
            def _():
                results_wait(c, 1, lag.at[pl.ds(0, ROW - 1), c]).wait_send()

        @pl.when(jnp.logical_not(sums))
        def _():
            mate_send(c).wait_send()

    def results_arrived(c):
        @pl.when(x != tm)
        def _():
            results_wait(c, 0, from_row.at[:, c]).wait_recv()

        @pl.when(x == tm)
        def _():
            results_wait(c, 0, from_row.at[pl.ds(0, 1), c]).wait_recv()

        @pl.when(jnp.logical_and(has_after, x < 2))
        def _():
            results_wait(c, 1, from_next.at[:, c, pl.ds(16, 16)]).wait_recv()

        @pl.when(jnp.logical_and(has_after, x >= 2))
        def _():
            results_wait(c, 1, from_next.at[:, c]).wait_recv()

    @pl.when(jnp.logical_not(has_before))
    def _():
        @pl.loop(0, CHUNKS)
        def _(c):
            up[c] = jnp.zeros(up.shape[1:], up.dtype)

    @pl.when(jnp.logical_not(has_after))
    def _():
        @pl.loop(0, CHUNKS)
        def _(c):
            down[c] = jnp.zeros(down.shape[1:], down.dtype)

    def x_start(u, half=None):
        for d in (2, 1, 3):
            x_send(u, d, half).start()

    early = PIECES // 2 + 1
    whiten(0, 0)
    inv_copy.start()
    for c in range(1, CHUNKS):
        rec_copy(c).start()
    pl.semaphore_wait(barrier, peers)
    for u in range(early):
        x_start(u, 0)
    whiten(0, 1)
    for u in range(early):
        x_start(u, 1)
    for u in range(early, PIECES):
        x_start(u)
    inv_copy.wait()

    @pl.loop(0, UNITS + USE)
    def _(u):
        @pl.when(u < UNITS)
        def _():
            x_arrived(u)
            halo_start(u)

        @pl.when(jnp.logical_and(u >= PASS, u < UNITS + PASS))
        def _():
            pass_on(u - PASS)

        ahead, part = u // 2 + 1, lax.rem(u, 2)

        @pl.when(ahead < CHUNKS)
        def _():
            whiten(ahead, part)

        @pl.when(jnp.logical_and(ahead < CHUNKS, part == 1))
        def _():
            for p in range(PIECES):
                x_start(ahead * PIECES + p)

        @pl.when(u >= USE)
        def _():
            k = u - USE
            c, p = k // PIECES, lax.rem(k, PIECES)
            halo_arrived(k)
            correlate(c, p)

            @pl.when(p == PIECES - 1)
            def _():
                keep_results(c)

            @pl.when(jnp.logical_and(p == 0, c > 0))
            def _():
                send_results(c - 1)

    send_results(CHUNKS - 1)
    x_sent()
    halo_sent()
    for c in range(CHUNKS):
        results_arrived(c)
        inside = from_row[0, c].astype(F32) + from_row[1, c].astype(F32)
        beyond = from_next[0, c].astype(F32) + from_next[1, c].astype(F32)
        for offset in range(1, REACH + 1):
            within = jnp.logical_or(sub < 4, x + offset < ROW)
            at = (offset - 1) * 8
            tile = jnp.where(within, inside[at : at + 8], beyond[at : at + 8])
            out_ref[offset - 1, 8 * c : 8 * c + 8] = tile
    for c in range(CHUNKS):
        results_sent(c)


def body(records, partners):
    channels, windows, length = records.shape
    total_windows = windows * lax.axis_size("tm")
    scale = 1.0 / math.sqrt(total_windows * FREQ)
    dma = pltpu.SemaphoreType.DMA
    lagged = pl.pallas_call(
        functools.partial(kernel, scale),
        out_shape=jax.ShapeDtypeStruct((REACH, channels // TM, LAGS), F32),
        in_specs=[pl.BlockSpec(memory_space=pl.ANY)] * 3,
        out_specs=pl.BlockSpec(memory_space=pltpu.VMEM),
        scratch_shapes=[
            pltpu.VMEM((CHUNKS, ROW, 2, 4, windows, length), BF16),
            pltpu.VMEM((PIECES, DEEP, 2 * WIDE), BF16),
            pltpu.VMEM((PIECES, 2 * WIDE, 2 * LAGS), BF16),
            pltpu.VMEM((ROW, CHUNKS, PIECES, 2, 32, 2 * WIDE), BF16),
            pltpu.VMEM((CHUNKS, PIECES, 2, ROW, 32, 2 * WIDE), BF16),
            pltpu.VMEM((CHUNKS, PIECES, ROW, 32, 2 * WIDE), BF16),
            pltpu.VMEM((CHUNKS, PIECES, ROW, 32, 2 * WIDE), BF16),
            pltpu.VMEM((2, CHUNKS, PIECES, 2, 32, 2 * WIDE), BF16),
            pltpu.VMEM((128, 2 * WIDE), F32),
            pltpu.VMEM((128, LAGS), F32),
            pltpu.VMEM((CHUNKS, 128, LAGS), F32),
            pltpu.VMEM((CHUNKS, 128, LAGS), F32),
            pltpu.VMEM((ROW, CHUNKS, 32, LAGS), RESULT),
            pltpu.VMEM((TM // 2, CHUNKS, 32, LAGS), RESULT),
            pltpu.VMEM((TM // 2, CHUNKS, 32, LAGS), RESULT),
            dma((CHUNKS,)), dma((PIECES,)), dma,
            dma, dma((UNITS,)),
            dma((2,)), dma((UNITS, 2)),
            dma((2,)), dma((UNITS, 2)),
            dma((CHUNKS,)), dma((CHUNKS,)),
            dma((CHUNKS, 2)), dma((CHUNKS, 2)),
        ],
        compiler_params=pltpu.CompilerParams(
            collective_id=0, has_side_effects=True, vmem_limit_bytes=56 << 20
        ),
        cost_estimate=pl.CostEstimate(
            flops=7 * 10**9, bytes_accessed=12 * 10**6, transcendentals=10**6
        ),
    )(
        records.reshape(ROW, CHUNKS, 2, channels // (ROW * CHUNKS * 2), windows, length),
        jnp.asarray(forward_matrix()),
        jnp.asarray(inverse_matrix()),
    )
    offsets = partners[0] - lax.axis_index("chan")
    chosen = 0.0
    for k in range(REACH):
        chosen = chosen + jnp.where((offsets == k + 1)[:, None, None], lagged[k][None], 0.0)
    return chosen[None]


def solution(mesh):
    return jax.shard_map(
        body,
        mesh=mesh,
        in_specs=(P("chan", "tm", None), P("chan", None)),
        out_specs=P("chan", None, "tm", None),
        check_vma=False,
    )
```
